32 devices in a mesh: rep: 4 (over y, x), fsdp: 8 (over z, core).
Axes of the slice: x: 2, y: 2, z: 4, core: 2. Of those that a mesh axis runs over, the one named last changes fastest.
Arguments:
- states: bfloat16 [128, 32, 5120], P('fsdp'), may hold values from -6 to 6
- labels: bfloat16 [128, 8], P('fsdp'), may hold values from -4 to 4
- lengths: int32 [128], P('fsdp'), may hold values from 1 to 32
- segments: int32 [128, 32], P('fsdp'), may hold values from 0 to 7, never falling along the last dimension, each value on 1 to 8 neighbouring positions
- destinations: int32 [128, 1], P('fsdp'), may hold values from 0 to 7; in each aligned block of 16 rows (0 to 15, 16 to 31, ...) at most 2 rows name the same one
- gain: float32 [5120], replicated, may hold values from 0.1 to 1.9
- head_in: bfloat16 [5120, 5120], P('fsdp', 'rep'), may hold values from -0.078125 to 0.078125
- head_out: float32 [5120], P('rep'), may hold values from -0.078125 to 0.078125
Outputs:
- step_rewards: float32 [128, 8], P('fsdp')
- head_grad: float32 [5120, 5120], P('fsdp', 'rep')
The draws below stay inside these ranges and needn't reach their ends.
Inputs may be any that keep to these rules, and one draw needn't show every extreme that they name: `destinations`: among the 16 rows of one generator device no trainer index is named by more than 2 rows, a bound that some block reaches. `segments`: step numbers never fall along a row; every step has 1 to 8 slots, one step of each row exactly 8.
All inputs are finite; a program needn't handle non-finite values.
Results may differ from the reference program's by a relative error of at most 0.0052.
Values may be sent and summed in bfloat16 or wider, within the bound.
No kernel may reach another device: no remote copies, remote signals or barrier semaphores. Data moves between devices by JAX's collectives and lax.ppermute only.
A program may use at most 128 MiB of HBM per device.

```python
import math
import jax
import jax.numpy as jnp
import numpy as np
from jax import lax

D = 5120
H = 5120
R = 16
CAP = 2
S = 32
STEPS = 8
SEGMAX = 8
ROWS_ALL = 128
N_FSDP = 8


def place_ends(values, rng, low, top_value):
    longest = values.shape.index(max(values.shape))
    spots = []
    for shift in (0, 1):
        where = [jax.random.randint(jax.random.fold_in(rng, axis), (), 0, length) for axis, length in enumerate(values.shape)]
        where[longest] = (where[longest] + shift) % values.shape[longest]
        spots.append(tuple(where))
    return values.at[spots[0]].set(low).at[spots[1]].set(top_value)


def steps_of(stream_key, extent, cuts, least, high):
    level = 1.0
    for axis_at, parts in cuts:
        draws = jax.random.uniform(jax.random.fold_in(jax.random.fold_in(stream_key, 6), axis_at), (parts,), jnp.float32, least / len(cuts), high / len(cuts))
        level = level * jnp.repeat(jnp.exp(draws), extent[axis_at] // parts).reshape((-1,) + (1,) * (len(extent) - 1 - axis_at))
    return level


def split_up(number_of, total, bound, skew):
    portions = [(1 << 20) // math.isqrt(rank ** skew) + 1 for rank in range(2, number_of + 1)]
    rest, holding = total - bound - (number_of - 1), [1] * (number_of - 1)
    while rest > 0:
        movable = [i for i in range(number_of - 1) if holding[i] < bound]
        whole, remaining = sum([portions[i] for i in movable]), rest
        for i in movable:
            more = min(bound - holding[i], max(1, remaining * portions[i] // whole), rest)
            holding[i] = holding[i] + more
            rest = rest - more
    return np.array([bound] + holding)


def ragged_sizes(rng, amount, total, bound, lean):
    if amount == 2:
        one = jax.random.randint(rng, (), max(1, total - bound), min(bound, total - 1) + 1)
        return jnp.stack([one, total - one])
    tallies = jnp.asarray(split_up(amount, total, bound, lean), jnp.int32)
    couples = (amount - 1) // 2
    source_of, taker = tallies[1:1 + 2 * couples:2], tallies[2:2 + 2 * couples:2]
    slack = jnp.minimum(source_of - 1, bound - taker)
    moved = jax.random.randint(jax.random.fold_in(rng, 1), (couples,), 0, 1 << 20) % (slack + 1)
    tallies = tallies.at[1:1 + 2 * couples:2].set(source_of - moved).at[2:2 + 2 * couples:2].set(taker + moved)
    return tallies[jax.random.permutation(jax.random.fold_in(rng, 2), amount)]


def routed_block(rng, own, number, rows, count, top, bound, slope):
    sequence = jax.random.permutation(rng, count)
    heavy_load, ordinary = portions_of(count, rows * top, bound, slope, True), portions_of(count, rows * top, bound, slope, False)
    places = jnp.arange(count)

    def named(tallies, offset_by):
        used = int((tallies > 0).sum())
        fixed = max(1, used // 4)
        passed = fixed + (places - fixed + offset_by * (used - fixed)) % max(1, count - fixed)
        return jnp.zeros((count,), jnp.int32).at[sequence[jnp.where(places < fixed, places, passed)]].set(jnp.asarray(tallies, jnp.int32))

    tallies = jnp.where(number % 4 == 0, named(heavy_load, number // 4), named(ordinary, number - number // 4 - 1))
    mixed = jax.random.permutation(jax.random.fold_in(own, 3), count)
    source_of, taker = mixed[0:count // 2 * 2:2], mixed[1:count // 2 * 2:2]
    slack = jnp.minimum(tallies[source_of] - 1, bound - tallies[taker]) // 2
    slack = jnp.where((source_of == sequence[0]) | (taker == sequence[0]) | (tallies[taker] == 0), 0, jnp.maximum(slack, 0))
    passed = jax.random.randint(jax.random.fold_in(own, 4), (count // 2,), 0, 1 << 20) % (slack + 1)
    tallies = tallies.at[source_of].add(-passed).at[taker].add(passed)
    items = jnp.searchsorted(jnp.cumsum(tallies), jnp.arange(rows * top), side="right").astype(jnp.int32)
    table = items.reshape(top, rows).T
    table = table[jax.random.permutation(jax.random.fold_in(own, 1), rows)]
    offset_by = jax.random.randint(jax.random.fold_in(own, 2), (rows, 1), 0, top)
    return jnp.take_along_axis(table, (jnp.arange(top)[None, :] + offset_by) % top, axis=1)


def portions_of(number_of, total, bound, skew, full):
    weights = [(1 << 20) // math.isqrt(rank ** skew) + 1 for rank in range(1, number_of + 1)]
    largest = bound if full else min(bound, max(-(-total // number_of), total * weights[0] // sum(weights)))
    least = 1 if total - largest >= number_of - 1 else 0
    counts, spare = [largest] + [least] * (number_of - 1), total - largest - least * (number_of - 1)
    while spare > 0:
        free = [i for i in range(1, number_of) if counts[i] < largest] or [i for i in range(1, number_of) if counts[i] < bound]
        whole, remaining = sum([weights[i] for i in free]), spare
        for i in free:
            addition = min(bound - counts[i], max(1, remaining * weights[i] // whole), spare)
            counts[i] = counts[i] + addition
            spare = spare - addition
    return np.array(counts)


def normal_values(own_key, dims, deviation, limit, pieces=(), held_as=jnp.bfloat16):
    level = steps_of(own_key, dims, pieces, -0.22, 0.18) if pieces else 1.0
    array = jax.random.normal(own_key, dims, jnp.float32) * deviation * level
    return jnp.minimum(jnp.maximum(array, -limit), limit).astype(held_as)


def setup_inputs(seed: int = 0) -> dict:
    keys = jax.random.split(jax.random.key(seed), 9)
    states = normal_values(keys[0], (ROWS_ALL, S, D), 1.0, 6.0, ((0, 8),))
    labels = normal_values(keys[1], (ROWS_ALL, STEPS), 1.0, 4.0, ((0, 8),))
    lengths = place_ends(jax.random.randint(keys[2], (ROWS_ALL,), 1, S + 1), jax.random.fold_in(keys[2], 1), 1, S).astype(jnp.int32)
    segments = jax.vmap(lambda own: jnp.searchsorted(jnp.cumsum(ragged_sizes(own, STEPS, S, SEGMAX, 1)), jnp.arange(S), side="right"))(jax.random.split(keys[3], ROWS_ALL)).reshape((ROWS_ALL, S)).astype(jnp.int32)
    destinations_keys = jax.random.split(jax.random.fold_in(keys[4], 1), ROWS_ALL // R)
    destinations_turns = jax.random.permutation(jax.random.fold_in(keys[4], 3), ROWS_ALL // R)
    destinations = jax.vmap(lambda own, number: routed_block(jax.random.fold_in(keys[4], 2), own, number, R, N_FSDP, 1, CAP, 2))(destinations_keys, destinations_turns).reshape((ROWS_ALL, 1))
    gain = jnp.clip(1.0 + 0.18 * jax.random.normal(keys[5], (D,), jnp.float32), 0.1, 1.9)
    head_in = normal_values(keys[6], (D, H), D ** -0.5, 0.078125, ((0, 8), (1, 4)))
    head_out = normal_values(keys[7], (H,), H ** -0.5, 0.078125, ((0, 4),), jnp.float32)
    return {"states": states, "labels": labels, "lengths": lengths, "segments": segments, "destinations": destinations, "gain": gain, "head_in": head_in, "head_out": head_out}


def silu_slope(pre_act):
    sigma = jax.nn.sigmoid(pre_act)
    return sigma * (1.0 + pre_act * (1.0 - sigma))

def normalize(tokens_flat, gain):
    wide = tokens_flat.astype(jnp.float32)
    meansq = lax.optimization_barrier(jnp.mean(wide * wide, axis=1, keepdims=True))
    return (wide * lax.rsqrt(meansq + 1e-06) * gain[None, :]).astype(jnp.bfloat16)

def reference(states, labels, lengths, segments, destinations, gain, head_in, head_out):
    total_rows = states.shape[0]
    normed = normalize(states.reshape(-1, D), gain)
    positions = jnp.arange(S, dtype=jnp.int32)
    valid = (positions[None, :] < lengths[:, None]).astype(jnp.float32)
    step_ids = jnp.arange(STEPS, dtype=jnp.int32)
    member = (segments[:, :, None] == step_ids[None, None, :]).astype(jnp.float32) * valid[:, :, None]
    live = lax.optimization_barrier(jnp.max(member, axis=1))
    pre_act = jnp.dot(normed, head_in, preferred_element_type=jnp.float32)
    score = lax.optimization_barrier(jnp.sum(jax.nn.silu(pre_act) * head_out[None, :], axis=1)).reshape(total_rows, S)
    step_score = jnp.einsum('rs,rsk->rk', score, member, precision=lax.Precision.HIGHEST)
    step_error = live * (step_score - labels.astype(jnp.float32))
    token_error = jnp.einsum('rk,rsk->rs', step_error, member, precision=lax.Precision.HIGHEST).reshape(-1)
    pre_grad = (token_error[:, None] * head_out[None, :] * silu_slope(pre_act)).astype(jnp.bfloat16)
    head_grad = jnp.dot(normed.T, pre_grad, preferred_element_type=jnp.float32)
    rate = 0.5 / math.sqrt(total_rows * S)
    fresh = (head_in.astype(jnp.float32) - rate * head_grad).astype(jnp.bfloat16)
    pre_fresh = jnp.dot(normed, fresh, preferred_element_type=jnp.float32)
    fresh_score = lax.optimization_barrier(jnp.sum(jax.nn.silu(pre_fresh) * head_out[None, :], axis=1)).reshape(total_rows, S)
    reward = jnp.einsum('rs,rsk->rk', fresh_score, member, precision=lax.Precision.HIGHEST)
    target = destinations[:, 0].astype(jnp.int32)
    order = jnp.arange(total_rows, dtype=jnp.int32)
    block_id = order // R
    earlier = (target[:, None] == target[None, :]) & (block_id[:, None] == block_id[None, :]) & (order[None, :] < order[:, None])
    rank_in = lax.optimization_barrier(jnp.sum(earlier.astype(jnp.int32), axis=1))
    target_row = target * (N_FSDP * CAP) + block_id * CAP + rank_in
    step_rewards = jnp.zeros((N_FSDP * N_FSDP * CAP, STEPS), jnp.float32).at[target_row].set(reward)
    return (step_rewards, head_grad)
```

```python
import math

import jax
import jax.numpy as jnp
from jax import lax
from jax.sharding import PartitionSpec as P

CAP = 2
STEPS = 8
CHUNKS = 2


def silu_slope(pre_act):
    sigma = jax.nn.sigmoid(pre_act)
    return sigma * (1.0 + pre_act * (1.0 - sigma))


def normalize(tokens_flat, gain):
    wide = tokens_flat.astype(jnp.float32)
    meansq = jnp.mean(wide * wide, axis=1, keepdims=True)
    return (wide * lax.rsqrt(meansq + 1e-06) * gain[None, :]).astype(jnp.bfloat16)


def member_of(segments, lengths):
    positions = jnp.arange(segments.shape[1], dtype=jnp.int32)
    valid = (positions[None, :] < lengths[:, None]).astype(jnp.float32)
    step_ids = jnp.arange(STEPS, dtype=jnp.int32)
    return (segments[:, :, None] == step_ids[None, None, :]).astype(jnp.float32) * valid[:, :, None]


def rank_of(target):
    order = jnp.arange(target.shape[0], dtype=jnp.int32)
    earlier = (target[:, None] == target[None, :]) & (order[None, :] < order[:, None])
    return jnp.sum(earlier.astype(jnp.int32), axis=1)


def gathered_weights(states, labels, lengths, segments, destinations, gain, head_in, head_out):
    row_count, slot_span, feature_width = states.shape
    trainers = lax.axis_size("fsdp")
    slot_total = trainers * CAP
    normed = normalize(states.reshape(-1, feature_width), gain)
    member = member_of(segments, lengths)
    live = jnp.max(member, axis=1)

    def scored(weights):
        pre_act = jnp.dot(normed, weights, preferred_element_type=jnp.float32)
        partial = jnp.sum(jax.nn.silu(pre_act) * head_out[None, :], axis=1)
        return pre_act, lax.psum(partial, "rep").reshape(row_count, slot_span)

    pre_act, score = scored(lax.all_gather(head_in, "fsdp", axis=0, tiled=True))
    step_score = jnp.einsum("rs,rsk->rk", score, member, precision=lax.Precision.HIGHEST)
    step_error = live * (step_score - labels.astype(jnp.float32))
    token_error = jnp.einsum("rk,rsk->rs", step_error, member, precision=lax.Precision.HIGHEST).reshape(-1)
    pre_grad = (token_error[:, None] * head_out[None, :] * silu_slope(pre_act)).astype(jnp.bfloat16)
    rate = 0.5 / math.sqrt(row_count * trainers * slot_span)
    head_grad = lax.psum_scatter(
        lax.dot_general(normed, pre_grad, (((0,), (0,)), ((), ())), preferred_element_type=jnp.float32),
        "fsdp",
        scatter_dimension=0,
        tiled=True,
    )
    fresh = (head_in.astype(jnp.float32) - rate * head_grad).astype(jnp.bfloat16)
    _, fresh_score = scored(lax.all_gather(fresh, "fsdp", axis=0, tiled=True))
    reward = jnp.einsum("rs,rsk->rk", fresh_score, member, precision=lax.Precision.HIGHEST)
    target = destinations[:, 0]
    slot = target * CAP + rank_of(target)
    placing = (slot[None, :] == jnp.arange(slot_total, dtype=jnp.int32)[:, None]).astype(jnp.float32)
    placed = jnp.dot(placing, reward, precision=lax.Precision.HIGHEST)
    return lax.all_to_all(placed, "fsdp", split_axis=0, concat_axis=0, tiled=True), head_grad


X_MATE = [(r, r ^ 1) for r in range(4)]
Y_MATE = [(r, r ^ 2) for r in range(4)]
XY_MATE = [(r, r ^ 3) for r in range(4)]
CORE_MATE = [(f, f ^ 1) for f in range(8)]
Z1_MATE = [(f, f ^ 2) for f in range(8)]
Z2_MATE = [(f, f ^ 4) for f in range(8)]
Z3_MATE = [(f, f ^ 6) for f in range(8)]
INNER = [(f, f ^ 6) for f in (2, 3, 4, 5)]
OUTWARD = [(f, f ^ 2) for f in (2, 3, 4, 5)]


def sum_everywhere(values):
    values = values + lax.ppermute(values, "fsdp", CORE_MATE)
    values = (values + lax.ppermute(values, "rep", X_MATE)) + (
        lax.ppermute(values, "rep", Y_MATE) + lax.ppermute(values, "rep", XY_MATE)
    )
    return (values + lax.ppermute(values, "fsdp", Z1_MATE)) + (
        lax.ppermute(values, "fsdp", Z2_MATE) + lax.ppermute(values, "fsdp", Z3_MATE)
    )


def gather_small(values):
    f = lax.axis_index("fsdp")
    mates = [values] + [
        lax.ppermute(values, "fsdp", [(i, i ^ j) for i in range(8)]) for j in range(1, 8)
    ]
    stacked = jnp.stack(mates)
    order = jnp.arange(8, dtype=jnp.int32) ^ f
    return jnp.sum(
        jnp.where((order[:, None] == jnp.arange(8)[None, :])[:, :, None], stacked[None], 0.0), axis=1
    )


def spread_tokens(local, states, labels, lengths, segments, destinations, gain, head_in, head_out):
    row_count, slot_span, width = states.shape
    f = lax.axis_index("fsdp")
    r = lax.axis_index("rep")
    z = f // 2
    c = f % 2
    inner = (z == 1) | (z == 2)
    hidden = head_in.shape[1] // 8
    depth = head_in.shape[0]

    counts = jnp.sum(member_of(segments, lengths), axis=1)
    target = destinations[:, 0]
    slot_of = target * (8 * CAP) + f * CAP + rank_of(target)
    facts = jnp.concatenate(
        [counts.reshape(-1), labels.astype(jnp.float32).reshape(-1), slot_of.astype(jnp.float32)]
    )
    facts = jnp.pad(facts, (0, 384 - facts.shape[0]))
    facts_all = gather_small(facts)
    steps = row_count * STEPS
    counts_all = facts_all[:, :steps]
    labels_all = facts_all[:, steps : 2 * steps]
    slots_all = facts_all[:, 2 * steps : 2 * steps + row_count].reshape(-1)
    live_all = jnp.minimum(counts_all, 1.0)
    upto = jnp.arange(steps)[:, None] >= jnp.arange(steps)[None, :]
    ends_all = jnp.sum(jnp.where(upto[None], counts_all[:, None, :], 0.0), axis=2)

    ends_row = jnp.sum(
        jnp.where(
            jnp.arange(row_count)[:, None] >= jnp.arange(row_count)[None, :], lengths[None, :], 0
        ),
        axis=1,
    )
    place = jnp.where(
        jnp.arange(slot_span)[None, :] < lengths[:, None],
        (ends_row - lengths)[:, None] + jnp.arange(slot_span)[None, :],
        -1,
    ).reshape(-1)
    picks = (place[None, :] == jnp.arange(local, dtype=jnp.int32)[:, None]).astype(jnp.bfloat16)
    tokens = jnp.dot(picks, states.reshape(-1, width), preferred_element_type=jnp.float32)
    own = normalize(tokens.astype(jnp.bfloat16), gain)

    head_pieces = jnp.transpose(head_in).reshape(8, hidden, depth)
    head_got = lax.all_to_all(head_pieces, "fsdp", split_axis=0, concat_axis=0, tiled=True)
    head_t = jnp.transpose(head_got.reshape(8, hidden, depth), (1, 0, 2)).reshape(hidden, width)
    out_share = lax.dynamic_slice_in_dim(head_out, f * hidden, hidden)[:, None]

    quarter = local // 4
    piece = quarter // CHUNKS
    half = piece // 16 * 8
    mine = lax.dynamic_slice_in_dim(own, r * quarter, quarter)
    groups = [[own, lax.ppermute(own, "fsdp", CORE_MATE)]]
    arrived = {"a": [], "b": [], "c": []}

    def in_plane(part):
        from_x = lax.ppermute(part, "rep", X_MATE)
        from_y = lax.ppermute(part, "rep", Y_MATE)
        diag_low = lax.ppermute(from_x[:half], "rep", Y_MATE)
        diag_high = lax.ppermute(from_y[half:], "rep", X_MATE)
        return jnp.concatenate([part, from_x, from_y, diag_low, diag_high])

    for chunk in range(CHUNKS):
        part = mine[chunk * piece : (chunk + 1) * piece]
        first = lax.ppermute(part, "fsdp", Z1_MATE)
        first_in = lax.ppermute(part, "fsdp", INNER)
        second_out = lax.ppermute(first_in, "fsdp", OUTWARD)
        second_in = lax.ppermute(first, "fsdp", INNER)
        third_out = lax.ppermute(second_in, "fsdp", OUTWARD)
        for name, got in (
            ("a", first),
            ("b", jnp.where(inner, first_in, second_out)),
            ("c", jnp.where(inner, second_in, third_out)),
        ):
            full = in_plane(got)
            arrived[name].append(full)
            arrived[name].append(lax.ppermute(full, "fsdp", CORE_MATE))
    for name in "abc":
        groups.append(arrived[name])
    groups = [jnp.concatenate(parts) for parts in groups]

    lower = z < 2
    sources = [z, z ^ 1, jnp.where(lower, 2, 1), jnp.where(lower, 3, 0)]
    place_own = jnp.arange(local, dtype=jnp.int32)
    in_piece = jnp.arange(piece, dtype=jnp.int32)
    place_chunks = [
        jnp.concatenate([(r ^ j) * quarter + chunk * piece + in_piece for j in range(4)])
        for chunk in range(CHUNKS)
    ]

    def step_bounds(source, core):
        take = jnp.arange(8) == source * 2 + core
        ends = jnp.sum(jnp.where(take[:, None], ends_all, 0.0), axis=0)
        counts_here = jnp.sum(jnp.where(take[:, None], counts_all, 0.0), axis=0)
        return ends - counts_here, ends

    marks = []
    for index in range(4):
        cores = []
        for core in (c, 1 - c):
            low, high = step_bounds(sources[index], core)
            cores.append((low, high))
        rows = []
        if index == 0:
            rows = [(place_own, 0), (place_own, 1)]
        else:
            for chunk in range(CHUNKS):
                rows += [(place_chunks[chunk], 0), (place_chunks[chunk], 1)]
        masks = [
            (spot[None, :].astype(jnp.float32) >= cores[which][0][:, None])
            & (spot[None, :].astype(jnp.float32) < cores[which][1][:, None])
            for spot, which in rows
        ]
        marks.append((rows, masks))

    def onto_steps(scores):
        total = jnp.zeros((8, steps), jnp.float32)
        for index in range(4):
            rows, masks = marks[index]
            sums = [jnp.zeros((steps,), jnp.float32)] * 2
            at = 0
            for (spot, which), mask in zip(rows, masks):
                span = spot.shape[0]
                piece_score = scores[index][at : at + span]
                sums[which] = sums[which] + jnp.sum(jnp.where(mask, piece_score[None, :], 0.0), axis=1)
                at += span
            for which, core in ((0, c), (1, 1 - c)):
                take = jnp.arange(8) == sources[index] * 2 + core
                total = total + jnp.where(take[:, None], sums[which][None, :], 0.0)
        return total

    def onto_tokens(values):
        spread = []
        for index in range(4):
            rows, masks = marks[index]
            here = []
            for core in (c, 1 - c):
                take = jnp.arange(8) == sources[index] * 2 + core
                here.append(jnp.sum(jnp.where(take[:, None], values, 0.0), axis=0))
            spread.append(
                jnp.concatenate(
                    [
                        jnp.sum(jnp.where(mask, here[which][:, None], 0.0), axis=0)
                        for (spot, which), mask in zip(rows, masks)
                    ]
                )
            )
        return spread

    def forward(weights_t):
        return [
            lax.dot_general(
                weights_t, group, (((1,), (1,)), ((), ())), preferred_element_type=jnp.float32
            )
            for group in groups
        ]

    pres = forward(head_t)
    part_scores = [jnp.sum(jax.nn.silu(pre) * out_share, axis=0) for pre in pres]
    step_score = sum_everywhere(onto_steps(part_scores))
    step_error = live_all * (step_score - labels_all)
    errors = onto_tokens(step_error)
    grad_t = jnp.zeros((hidden, width), jnp.float32)
    for pre, error, group in zip(pres, errors, groups):
        pre_grad = (error[None, :] * out_share * silu_slope(pre)).astype(jnp.bfloat16)
        grad_t = grad_t + jnp.dot(pre_grad, group, preferred_element_type=jnp.float32)
    rate = 0.5 / math.sqrt(row_count * 8 * slot_span)
    fresh_t = (head_t.astype(jnp.float32) - rate * grad_t).astype(jnp.bfloat16)

    grad_pieces = jnp.transpose(grad_t.astype(jnp.bfloat16).reshape(hidden, 8, depth), (1, 0, 2))
    grad_got = lax.all_to_all(grad_pieces, "fsdp", split_axis=0, concat_axis=0, tiled=True)
    head_grad = jnp.transpose(grad_got.reshape(8 * hidden, depth)).astype(jnp.float32)

    fresh_scores = [jnp.sum(jax.nn.silu(pre) * out_share, axis=0) for pre in forward(fresh_t)]
    reward = sum_everywhere(onto_steps(fresh_scores)).reshape(8 * row_count, STEPS)
    wanted = f * (8 * CAP) + jnp.arange(8 * CAP, dtype=jnp.int32)
    hits = slots_all[None, :] == wanted[:, None].astype(jnp.float32)
    step_rewards = jnp.sum(jnp.where(hits[:, :, None], reward[None], 0.0), axis=1)
    return step_rewards, head_grad


def solution(mesh):
    in_specs = (
        P("fsdp", None, None),
        P("fsdp", None),
        P("fsdp"),
        P("fsdp", None),
        P("fsdp", None),
        P(),
        P("fsdp", "rep"),
        P("rep"),
    )
    out_specs = (P("fsdp", None), P("fsdp", "rep"))

    def local(states, *rest):
        if lax.axis_size("rep") == 4 and lax.axis_size("fsdp") == 8:
            return spread_tokens(states.shape[0] * states.shape[1], states, *rest)
        return gathered_weights(states, *rest)

    return jax.shard_map(local, mesh=mesh, in_specs=in_specs, out_specs=out_specs, check_vma=False)
```

```python
import math

import jax
import jax.numpy as jnp
from jax import lax
from jax.sharding import PartitionSpec as P

CAP = 2
STEPS = 8
LOCAL = 352


def silu_slope(pre_act):
    sigma = jax.nn.sigmoid(pre_act)
    return sigma * (1.0 + pre_act * (1.0 - sigma))


def normalize(tokens_flat, gain):
    wide = tokens_flat.astype(jnp.float32)
    meansq = jnp.mean(wide * wide, axis=1, keepdims=True)
    return (wide * lax.rsqrt(meansq + 1e-06) * gain[None, :]).astype(jnp.bfloat16)


def member_of(segments, lengths):
    positions = jnp.arange(segments.shape[1], dtype=jnp.int32)
    valid = (positions[None, :] < lengths[:, None]).astype(jnp.float32)
    step_ids = jnp.arange(STEPS, dtype=jnp.int32)
    return (segments[:, :, None] == step_ids[None, None, :]).astype(jnp.float32) * valid[:, :, None]


def rank_of(target):
    order = jnp.arange(target.shape[0], dtype=jnp.int32)
    earlier = (target[:, None] == target[None, :]) & (order[None, :] < order[:, None])
    return jnp.sum(earlier.astype(jnp.int32), axis=1)


def gathered_weights(states, labels, lengths, segments, destinations, gain, head_in, head_out):
    row_count, slot_span, feature_width = states.shape
    trainers = lax.axis_size("fsdp")
    slot_total = trainers * CAP
    normed = normalize(states.reshape(-1, feature_width), gain)
    member = member_of(segments, lengths)
    live = jnp.max(member, axis=1)

    def scored(weights):
        pre_act = jnp.dot(normed, weights, preferred_element_type=jnp.float32)
        partial = jnp.sum(jax.nn.silu(pre_act) * head_out[None, :], axis=1)
        return pre_act, lax.psum(partial, "rep").reshape(row_count, slot_span)

    pre_act, score = scored(lax.all_gather(head_in, "fsdp", axis=0, tiled=True))
    step_score = jnp.einsum("rs,rsk->rk", score, member, precision=lax.Precision.HIGHEST)
    step_error = live * (step_score - labels.astype(jnp.float32))
    token_error = jnp.einsum("rk,rsk->rs", step_error, member, precision=lax.Precision.HIGHEST).reshape(-1)
    pre_grad = (token_error[:, None] * head_out[None, :] * silu_slope(pre_act)).astype(jnp.bfloat16)
    rate = 0.5 / math.sqrt(row_count * trainers * slot_span)
    head_grad = lax.psum_scatter(
        lax.dot_general(normed, pre_grad, (((0,), (0,)), ((), ())), preferred_element_type=jnp.float32),
        "fsdp",
        scatter_dimension=0,
        tiled=True,
    )
    fresh = (head_in.astype(jnp.float32) - rate * head_grad).astype(jnp.bfloat16)
    _, fresh_score = scored(lax.all_gather(fresh, "fsdp", axis=0, tiled=True))
    reward = jnp.einsum("rs,rsk->rk", fresh_score, member, precision=lax.Precision.HIGHEST)
    target = destinations[:, 0]
    slot = target * CAP + rank_of(target)
    placing = (slot[None, :] == jnp.arange(slot_total, dtype=jnp.int32)[:, None]).astype(jnp.float32)
    placed = jnp.dot(placing, reward, precision=lax.Precision.HIGHEST)
    return lax.all_to_all(placed, "fsdp", split_axis=0, concat_axis=0, tiled=True), head_grad


X_MATE = [(r, r ^ 1) for r in range(4)]
Y_MATE = [(r, r ^ 2) for r in range(4)]
XY_MATE = [(r, r ^ 3) for r in range(4)]
CORE_MATE = [(f, f ^ 1) for f in range(8)]
Z1_MATE = [(f, f ^ 2) for f in range(8)]
Z2_MATE = [(f, f ^ 4) for f in range(8)]
Z3_MATE = [(f, f ^ 6) for f in range(8)]
INNER = [(f, f ^ 6) for f in (2, 3, 4, 5)]
OUTWARD = [(f, f ^ 2) for f in (2, 3, 4, 5)]


def sum_over_chips(values):
    values = (values + lax.ppermute(values, "rep", X_MATE)) + (
        lax.ppermute(values, "rep", Y_MATE) + lax.ppermute(values, "rep", XY_MATE)
    )
    return (values + lax.ppermute(values, "fsdp", Z1_MATE)) + (
        lax.ppermute(values, "fsdp", Z2_MATE) + lax.ppermute(values, "fsdp", Z3_MATE)
    )


def core_swap(values):
    return lax.ppermute(values, "fsdp", CORE_MATE)


def gather_small(values):
    f = lax.axis_index("fsdp")
    mates = [values] + [
        lax.ppermute(values, "fsdp", [(i, i ^ j) for i in range(8)]) for j in range(1, 8)
    ]
    stacked = jnp.stack(mates)
    order = jnp.arange(8, dtype=jnp.int32) ^ f
    return jnp.sum(
        jnp.where((order[:, None] == jnp.arange(8)[None, :])[:, :, None], stacked[None], 0.0), axis=1
    )


def around(part, inner, beside=None):
    half = part.shape[0] // 16 * 8

    def along(values, pairs):
        return lax.ppermute(values, "fsdp", pairs)

    def x_of(values):
        return lax.ppermute(values, "rep", X_MATE)

    def y_of(values):
        return lax.ppermute(values, "rep", Y_MATE)

    together = lax.optimization_barrier
    a, b_in = together((along(part, Z1_MATE), along(part, INNER)))
    ax, ay, b_out, c_in = together((x_of(a), y_of(a), along(b_in, OUTWARD), along(a, INNER)))
    if beside is not None:
        beside, ax = together((beside, ax))
    b = jnp.where(inner, b_in, b_out)
    a_low, a_high, bx, by, c_out = together(
        (y_of(ax[:half]), x_of(ay[half:]), x_of(b), y_of(b), along(c_in, OUTWARD))
    )
    c = jnp.where(inner, c_in, c_out)
    b_low, b_high, cx, cy = together((y_of(bx[:half]), x_of(by[half:]), x_of(c), y_of(c)))
    c_low, c_high = y_of(cx[:half]), x_of(cy[half:])
    return [a, ax, ay, a_low, a_high, b, bx, by, b_low, b_high, c, cx, cy, c_low, c_high], beside


def spread_tokens(states, labels, lengths, segments, destinations, gain, head_in, head_out):
    row_count, slot_span, width = states.shape
    tokens_most = row_count * slot_span
    f = lax.axis_index("fsdp")
    r = lax.axis_index("rep")
    z = f // 2
    c = f % 2
    inner = (z == 1) | (z == 2)
    hidden = head_in.shape[1] // 8
    depth = head_in.shape[0]
    flat_states = states.reshape(-1, width)

    row_ids = jnp.arange(row_count)
    ends_row = jnp.sum(jnp.where(row_ids[:, None] >= row_ids[None, :], lengths[None, :], 0), axis=1)
    place = jnp.where(
        jnp.arange(slot_span)[None, :] < lengths[:, None],
        (ends_row - lengths)[:, None] + jnp.arange(slot_span)[None, :],
        -1,
    ).reshape(-1)

    def compacted(first, count):
        spots = first + jnp.arange(count, dtype=jnp.int32)
        picks = (place[None, :] == spots[:, None]).astype(jnp.bfloat16)
        tokens = jnp.dot(picks, flat_states, preferred_element_type=jnp.float32)
        return normalize(tokens.astype(jnp.bfloat16), gain)

    def gathered(first, count, beside=None):
        quarter = count // 4
        mine = compacted(first + r * quarter, quarter)
        parts, beside = around(mine, inner, beside)
        own = compacted(first, count)
        offsets = [first + (r ^ j) * quarter + jnp.arange(quarter) for j in range(4)]
        order = [(0, [first + jnp.arange(count)]), (1, offsets), (2, offsets), (3, offsets)]
        return jnp.concatenate([own] + parts), order, beside

    head_pieces = jnp.transpose(head_in).reshape(8, hidden, depth)
    main, main_order, head_pieces = gathered(0, LOCAL, head_pieces)

    counts = jnp.sum(member_of(segments, lengths), axis=1)
    target = destinations[:, 0]
    slot_of = target * (8 * CAP) + f * CAP + rank_of(target)
    facts = jnp.concatenate(
        [counts.reshape(-1), labels.astype(jnp.float32).reshape(-1), slot_of.astype(jnp.float32)]
    )
    facts = jnp.pad(facts, (0, 384 - facts.shape[0]))
    facts_all = gather_small(facts)
    steps = row_count * STEPS
    counts_all = facts_all[:, :steps]
    labels_all = facts_all[:, steps : 2 * steps]
    slots_all = facts_all[:, 2 * steps : 2 * steps + row_count].reshape(-1)
    live_all = jnp.minimum(counts_all, 1.0)
    upto = jnp.arange(steps)[:, None] >= jnp.arange(steps)[None, :]
    ends_all = jnp.sum(jnp.where(upto[None], counts_all[:, None, :], 0.0), axis=2)
    lows_all = ends_all - counts_all
    overflow = jnp.max(ends_all[:, steps - 1]) > LOCAL

    head_got = lax.all_to_all(head_pieces, "fsdp", split_axis=0, concat_axis=0, tiled=True)
    head_mine = jnp.transpose(head_got.reshape(8, hidden, depth), (1, 0, 2)).reshape(hidden, width)

    def both_cores(mine):
        theirs = core_swap(mine)
        return jnp.concatenate([jnp.where(c == 0, mine, theirs), jnp.where(c == 0, theirs, mine)])

    head_t = both_cores(head_mine)
    out_share = lax.dynamic_slice_in_dim(head_out, z * 2 * hidden, 2 * hidden)[:, None]
    rate = 0.5 / math.sqrt(row_count * 8 * slot_span)

    sources = [z, z ^ 1, jnp.where(z < 2, 2, 1), jnp.where(z < 2, 3, 0)]
    takes = [jnp.arange(8) == source * 2 + c for source in sources]

    def masks_of(order):
        masks = []
        for chip, offsets in order:
            spots = jnp.concatenate(offsets).astype(jnp.float32)[None, :]
            low = jnp.sum(jnp.where(takes[chip][:, None], lows_all, 0.0), axis=0)[:, None]
            high = jnp.sum(jnp.where(takes[chip][:, None], ends_all, 0.0), axis=0)[:, None]
            masks.append((chip, (spots >= low) & (spots < high)))
        return masks

    def onto_steps(parts):
        sums = [jnp.zeros((steps,), jnp.float32)] * 4
        for masks, scores in parts:
            at = 0
            for chip, mask in masks:
                span = scores[at : at + mask.shape[1]]
                sums[chip] = sums[chip] + jnp.sum(jnp.where(mask, span[None, :], 0.0), axis=1)
                at += mask.shape[1]
        return sum(jnp.where(take[:, None], got[None, :], 0.0) for take, got in zip(takes, sums))

    def onto_tokens(masks, values):
        here = [jnp.sum(jnp.where(take[:, None], values, 0.0), axis=0)[:, None] for take in takes]
        return jnp.concatenate(
            [jnp.sum(jnp.where(mask, here[chip], 0.0), axis=0) for chip, mask in masks]
        )

    def forward(weights_t, tokens):
        return lax.dot_general(
            weights_t, tokens, (((1,), (1,)), ((), ())), preferred_element_type=jnp.float32
        )

    def scored(pre):
        return jnp.sum(jax.nn.silu(pre) * out_share, axis=0)

    def rest_of(batches):
        step_score = sum_over_chips(onto_steps([(masks, scored(pre)) for _, masks, pre in batches]))
        step_error = live_all * (step_score - labels_all)
        grad_t = None
        for tokens, masks, pre in batches:
            error = onto_tokens(masks, step_error)
            pre_grad = (error[None, :] * out_share * silu_slope(pre)).astype(jnp.bfloat16)
            term = jnp.dot(pre_grad, tokens, preferred_element_type=jnp.float32)
            grad_t = term if grad_t is None else grad_t + term
        kept = lax.dynamic_slice_in_dim(grad_t, c * hidden, hidden)
        given = lax.dynamic_slice_in_dim(grad_t, (1 - c) * hidden, hidden)
        grad_mine = kept + core_swap(given)
        grad_pieces = jnp.transpose(
            grad_mine.astype(jnp.bfloat16).reshape(hidden, 8, depth), (1, 0, 2)
        )
        grad_got = lax.all_to_all(grad_pieces, "fsdp", split_axis=0, concat_axis=0, tiled=True)
        head_grad = jnp.transpose(grad_got.reshape(8 * hidden, depth)).astype(jnp.float32)
        fresh_t = both_cores((head_mine.astype(jnp.float32) - rate * grad_mine).astype(jnp.bfloat16))
        steps_here = onto_steps(
            [(masks, scored(forward(fresh_t, tokens))) for tokens, masks, _ in batches]
        )
        steps_here = steps_here + core_swap(steps_here)
        reward = sum_over_chips(steps_here).reshape(8 * row_count, STEPS)
        wanted = f * (8 * CAP) + jnp.arange(8 * CAP, dtype=jnp.int32)
        hits = slots_all[None, :] == wanted[:, None].astype(jnp.float32)
        return jnp.sum(jnp.where(hits[:, :, None], reward[None], 0.0), axis=1), head_grad

    main_batch = (main, masks_of(main_order), forward(head_t, main))
    if LOCAL == tokens_most:
        return rest_of([main_batch])

    def with_more():
        more, more_order, _ = gathered(LOCAL, tokens_most - LOCAL)
        return rest_of([main_batch, (more, masks_of(more_order), forward(head_t, more))])

    return lax.cond(overflow, with_more, lambda: rest_of([main_batch]))


def solution(mesh):
    in_specs = (
        P("fsdp", None, None),
        P("fsdp", None),
        P("fsdp"),
        P("fsdp", None),
        P("fsdp", None),
        P(),
        P("fsdp", "rep"),
        P("rep"),
    )
    out_specs = (P("fsdp", None), P("fsdp", "rep"))

    def local(states, *rest):
        if lax.axis_size("rep") == 4 and lax.axis_size("fsdp") == 8:
            return spread_tokens(states, *rest)
        return gathered_weights(states, *rest)

    return jax.shard_map(local, mesh=mesh, in_specs=in_specs, out_specs=out_specs, check_vma=False)
```

```python
import functools
import math

import jax
import jax.numpy as jnp
from jax import lax
from jax.experimental import pallas as pl
from jax.experimental.pallas import tpu as pltpu
from jax.sharding import PartitionSpec as P

CAP = 2
STEPS = 8
LOCAL = 384
VMEM_BYTES = 52 * 1024 * 1024


def silu_slope(pre_act):
    sigma = jax.nn.sigmoid(pre_act)
    return sigma * (1.0 + pre_act * (1.0 - sigma))


def normalize(tokens_flat, gain):
    wide = tokens_flat.astype(jnp.float32)
    meansq = jnp.mean(wide * wide, axis=1, keepdims=True)
    return (wide * lax.rsqrt(meansq + 1e-06) * gain[None, :]).astype(jnp.bfloat16)


def member_of(segments, lengths):
    positions = jnp.arange(segments.shape[1], dtype=jnp.int32)
    valid = (positions[None, :] < lengths[:, None]).astype(jnp.float32)
    step_ids = jnp.arange(STEPS, dtype=jnp.int32)
    return (segments[:, :, None] == step_ids[None, None, :]).astype(jnp.float32) * valid[:, :, None]


def rank_of(target):
    order = jnp.arange(target.shape[0], dtype=jnp.int32)
    earlier = (target[:, None] == target[None, :]) & (order[None, :] < order[:, None])
    return jnp.sum(earlier.astype(jnp.int32), axis=1)


def gathered_weights(states, labels, lengths, segments, destinations, gain, head_in, head_out):
    row_count, slot_span, feature_width = states.shape
    trainers = lax.axis_size("fsdp")
    slot_total = trainers * CAP
    normed = normalize(states.reshape(-1, feature_width), gain)
    member = member_of(segments, lengths)
    live = jnp.max(member, axis=1)

    def scored(weights):
        pre_act = jnp.dot(normed, weights, preferred_element_type=jnp.float32)
        partial = jnp.sum(jax.nn.silu(pre_act) * head_out[None, :], axis=1)
        return pre_act, lax.psum(partial, "rep").reshape(row_count, slot_span)

    pre_act, score = scored(lax.all_gather(head_in, "fsdp", axis=0, tiled=True))
    step_score = jnp.einsum("rs,rsk->rk", score, member, precision=lax.Precision.HIGHEST)
    step_error = live * (step_score - labels.astype(jnp.float32))
    token_error = jnp.einsum("rk,rsk->rs", step_error, member, precision=lax.Precision.HIGHEST).reshape(-1)
    pre_grad = (token_error[:, None] * head_out[None, :] * silu_slope(pre_act)).astype(jnp.bfloat16)
    rate = 0.5 / math.sqrt(row_count * trainers * slot_span)
    head_grad = lax.psum_scatter(
        lax.dot_general(normed, pre_grad, (((0,), (0,)), ((), ())), preferred_element_type=jnp.float32),
        "fsdp",
        scatter_dimension=0,
        tiled=True,
    )
    fresh = (head_in.astype(jnp.float32) - rate * head_grad).astype(jnp.bfloat16)
    _, fresh_score = scored(lax.all_gather(fresh, "fsdp", axis=0, tiled=True))
    reward = jnp.einsum("rs,rsk->rk", fresh_score, member, precision=lax.Precision.HIGHEST)
    target = destinations[:, 0]
    slot = target * CAP + rank_of(target)
    placing = (slot[None, :] == jnp.arange(slot_total, dtype=jnp.int32)[:, None]).astype(jnp.float32)
    placed = jnp.dot(placing, reward, precision=lax.Precision.HIGHEST)
    return lax.all_to_all(placed, "fsdp", split_axis=0, concat_axis=0, tiled=True), head_grad


X_MATE = [(r, r ^ 1) for r in range(4)]
Y_MATE = [(r, r ^ 2) for r in range(4)]
XY_MATE = [(r, r ^ 3) for r in range(4)]
CORE_MATE = [(f, f ^ 1) for f in range(8)]
Z1_MATE = [(f, f ^ 2) for f in range(8)]
Z2_MATE = [(f, f ^ 4) for f in range(8)]
Z3_MATE = [(f, f ^ 6) for f in range(8)]
INNER = [(f, f ^ 6) for f in (2, 3, 4, 5)]
OUTWARD = [(f, f ^ 2) for f in (2, 3, 4, 5)]


def sum_over_chips(values):
    values = (values + lax.ppermute(values, "rep", X_MATE)) + (
        lax.ppermute(values, "rep", Y_MATE) + lax.ppermute(values, "rep", XY_MATE)
    )
    return (values + lax.ppermute(values, "fsdp", Z1_MATE)) + (
        lax.ppermute(values, "fsdp", Z2_MATE) + lax.ppermute(values, "fsdp", Z3_MATE)
    )


def core_swap(values):
    return lax.ppermute(values, "fsdp", CORE_MATE)


def sum_in_turn(values):
    for axis, pairs in (("rep", X_MATE), ("rep", Y_MATE), ("fsdp", Z1_MATE), ("fsdp", Z2_MATE)):
        values = values + lax.ppermute(values, axis, pairs)
    return values


def gather_small(values):
    copies = jnp.broadcast_to(values[None], (8,) + values.shape)
    return lax.all_to_all(copies, "fsdp", split_axis=0, concat_axis=0, tiled=True)


def around(part, own, inner, weights=None, facts=None):
    half = part.shape[0] // 32 * 16
    together = lax.optimization_barrier

    def along(values, pairs):
        return lax.ppermute(values, "fsdp", pairs)

    def x_of(values):
        return lax.ppermute(values, "rep", X_MATE)

    def y_of(values):
        return lax.ppermute(values, "rep", Y_MATE)

    a, b_in = together((along(part, Z1_MATE), along(part, INNER)))
    own, a = together((own, a))
    second = (x_of(a), y_of(a), along(b_in, OUTWARD), along(a, INNER))
    if facts is not None:
        facts = gather_small(facts)
        second, facts = together((second, facts))
    ax, ay, b_out, c_in = together(second)
    b = jnp.where(inner, b_in, b_out)
    c_out = along(c_in, OUTWARD)
    a_low, a_high, bx, by = together((y_of(ax[:half]), x_of(ay[half:]), x_of(b), y_of(b)))
    c_out, bx = together((c_out, bx))
    if weights is not None:
        weights, c_out = together((weights, c_out))
        weights = lax.all_to_all(
            weights, "fsdp", 0, 0, axis_index_groups=[[0, 2, 4, 6], [1, 3, 5, 7]], tiled=True
        )
    c = jnp.where(inner, c_in, c_out)
    fourth = (y_of(bx[:half]), x_of(by[half:]), x_of(c), y_of(c))
    if weights is not None:
        fourth, weights = together((fourth, weights))
    b_low, b_high, cx, cy = together(fourth)
    c_low, c_high = y_of(cx[:half]), x_of(cy[half:])
    parts = [own, a, ax, ay, a_low, a_high, b, bx, by, b_low, b_high, c, cx, cy, c_low, c_high]
    return parts, weights, facts


def step_sums(pre, share, spots, bounds_ref, sums_ref, first):
    score = jnp.sum(pre * jax.nn.sigmoid(pre) * share, axis=0, keepdims=True)
    span = spots.shape[2]
    for at in range(2):
        chip = first + at
        here = spots[at]
        low = bounds_ref[chip, :, 0:1]
        high = bounds_ref[chip, :, 1:2]
        inside = (here >= low) & (here < high)
        sums = jnp.sum(jnp.where(inside, score[:, at * span : (at + 1) * span], 0.0), axis=1, keepdims=True)
        sums_ref[chip] = jnp.broadcast_to(sums, sums_ref.shape[1:])


def first_kernel(offsets_ref, *refs, sizes, blocks):
    count = len(sizes)
    parts = refs[:count]
    own_w, mate_w, share_ref, spots_ref, bounds_ref = refs[count : count + 5]
    pre_ref, sums_ref, kept_ref, given_ref, x_s, w_s, acc_s, in_sem, w_sem, out_sem = refs[count + 5 :]
    wide = own_w.shape[2]
    copies = []
    at = 0
    for index, size in enumerate(sizes):
        copies.append(pltpu.make_async_copy(parts[index], x_s.at[pl.ds(at, size)], in_sem.at[index]))
        at += size
    weight_copies = []
    for core, source in enumerate((own_w, mate_w)):
        for j in range(4):
            where = pl.ds(pl.multiple_of(offsets_ref[core * 4 + j], 128), wide)
            weight_copies.append(
                pltpu.make_async_copy(source.at[j], w_s.at[:, where], w_sem.at[core * 4 + j])
            )
    for copy in weight_copies + copies:
        copy.start()
    for copy in weight_copies:
        copy.wait()
    total = x_s.shape[0]
    tile = total // 2
    depth = x_s.shape[1] // blocks
    out_copies = []
    waited = 0
    at = 0
    for half in range(2):
        while at < (half + 1) * tile:
            copies[waited].wait()
            at += sizes[waited]
            waited += 1
        rows = pl.ds(half * tile, tile)
        for core, dest in enumerate((kept_ref, given_ref)):
            for j in range(4):
                where = pl.ds(pl.multiple_of(offsets_ref[core * 4 + j], 128), wide)
                out_copies.append(
                    pltpu.make_async_copy(
                        x_s.at[rows, where], dest.at[j, rows], out_sem.at[half * 8 + core * 4 + j]
                    )
                )
                out_copies[-1].start()
        acc_s[...] = jnp.zeros_like(acc_s)

        @pl.loop(0, blocks)
        def _(k):
            where = pl.ds(pl.multiple_of(k * depth, 128), depth)
            acc_s[...] += lax.dot_general(
                w_s[:, where], x_s[rows, where], (((1,), (1,)), ((), ())), preferred_element_type=jnp.float32
            )

        pre = acc_s[...]
        pre_ref[:, half * tile : (half + 1) * tile] = pre
        step_sums(pre, share_ref[...], spots_ref[half * 2 : half * 2 + 2], bounds_ref, sums_ref, half * 2)
    for copy in out_copies:
        copy.wait()


def first_scores(parts, own_w, mate_w, share, spots, bounds, offsets):
    sizes = tuple(part.shape[0] for part in parts)
    total = sum(sizes)
    width = parts[0].shape[1]
    units, wide = own_w.shape[1:]
    anywhere = pl.BlockSpec(memory_space=pl.ANY)
    vmem = pl.BlockSpec(memory_space=pltpu.VMEM)
    return pl.pallas_call(
        functools.partial(first_kernel, sizes=sizes, blocks=5),
        out_shape=(
            jax.ShapeDtypeStruct((units, total), jnp.float32),
            jax.ShapeDtypeStruct((4, bounds.shape[1], 128), jnp.float32),
            jax.ShapeDtypeStruct((4, total, wide), jnp.bfloat16),
            jax.ShapeDtypeStruct((4, total, wide), jnp.bfloat16),
        ),
        in_specs=[pl.BlockSpec(memory_space=pltpu.SMEM)] + [anywhere] * (len(parts) + 2) + [vmem] * 3,
        out_specs=(vmem, vmem, anywhere, anywhere),
        scratch_shapes=[
            pltpu.VMEM((total, width), jnp.bfloat16),
            pltpu.VMEM((units, width), jnp.bfloat16),
            pltpu.VMEM((units, total // 2), jnp.float32),
            pltpu.SemaphoreType.DMA((len(parts),)),
            pltpu.SemaphoreType.DMA((8,)),
            pltpu.SemaphoreType.DMA((16,)),
        ],
        compiler_params=pltpu.CompilerParams(vmem_limit_bytes=VMEM_BYTES),
        cost_estimate=pl.CostEstimate(
            flops=2 * units * width * total, bytes_accessed=4 * total * width, transcendentals=units * total
        ),
        name="first_scores",
    )(offsets, *parts, own_w, mate_w, share, spots, bounds)


def fresh_kernel(kept_ref, given_ref, own_w, mate_w, share_ref, spots_ref, bounds_ref, sums_ref, acc_s):
    half = pl.program_id(0)
    k = pl.program_id(1)
    contract = (((1,), (1,)), ((), ()))
    term = lax.dot_general(own_w[0], kept_ref[0], contract, preferred_element_type=jnp.float32)
    term = term + lax.dot_general(mate_w[0], given_ref[0], contract, preferred_element_type=jnp.float32)

    @pl.when(k == 0)
    def _():
        acc_s[...] = term

    @pl.when(k > 0)
    def _():
        acc_s[...] += term

    @pl.when(k == 3)
    def _():
        step_sums(acc_s[...], share_ref[...], spots_ref[...], bounds_ref, sums_ref, 0)


def fresh_scores(kept, given, own_w, mate_w, share, spots, bounds):
    total, wide = kept.shape[1:]
    units = own_w.shape[1]
    steps = bounds.shape[1]
    tile = total // 2
    tokens = pl.BlockSpec((1, tile, wide), lambda h, k: (k, h, 0))
    weights = pl.BlockSpec((1, units, wide), lambda h, k: (k, 0, 0))
    return pl.pallas_call(
        fresh_kernel,
        grid=(2, 4),
        out_shape=jax.ShapeDtypeStruct((4, steps, 128), jnp.float32),
        in_specs=[
            tokens,
            tokens,
            weights,
            weights,
            pl.BlockSpec((units, 1), lambda h, k: (0, 0)),
            pl.BlockSpec((2,) + spots.shape[1:], lambda h, k: (h, 0, 0)),
            pl.BlockSpec((2, steps, 2), lambda h, k: (h, 0, 0)),
        ],
        out_specs=pl.BlockSpec((2, steps, 128), lambda h, k: (h, 0, 0)),
        scratch_shapes=[pltpu.VMEM((units, tile), jnp.float32)],
        compiler_params=pltpu.CompilerParams(vmem_limit_bytes=VMEM_BYTES),
        cost_estimate=pl.CostEstimate(
            flops=4 * units * wide * 4 * total, bytes_accessed=16 * total * wide, transcendentals=units * total
        ),
        name="fresh_scores",
    )(kept, given, own_w, mate_w, share, spots, bounds)


def grad_kernel(rate, count, *refs):
    head_ref = refs[0]
    ins = refs[1 : 1 + 2 * count]
    grad_ref, fresh_ref = refs[1 + 2 * count :]
    grad = jnp.dot(ins[0][...], ins[1][0], preferred_element_type=jnp.float32)
    for at in range(2, 2 * count, 2):
        grad = grad + jnp.dot(ins[at][...], ins[at + 1][0], preferred_element_type=jnp.float32)
    grad_ref[0] = grad.astype(grad_ref.dtype)
    fresh_ref[0] = (head_ref[0].astype(jnp.float32) - rate * grad).astype(fresh_ref.dtype)


def grads_and_fresh(head, terms, rate):
    units, wide = head.shape[1:]
    block = pl.BlockSpec((1, units, wide), lambda j: (j, 0, 0))
    specs = [block]
    flat = [head]
    work = 0
    for pre_grad, tokens in terms:
        specs.append(pl.BlockSpec(pre_grad.shape, lambda j: (0, 0)))
        specs.append(pl.BlockSpec((1,) + tokens.shape[1:], lambda j: (j, 0, 0)))
        flat += [pre_grad, tokens]
        work += tokens.size
    return pl.pallas_call(
        functools.partial(grad_kernel, rate, len(terms)),
        grid=(4,),
        out_shape=(jax.ShapeDtypeStruct(head.shape, jnp.bfloat16),) * 2,
        in_specs=specs,
        out_specs=(block, block),
        compiler_params=pltpu.CompilerParams(vmem_limit_bytes=VMEM_BYTES),
        cost_estimate=pl.CostEstimate(flops=2 * units * work, bytes_accessed=2 * work, transcendentals=0),
        name="grads_and_fresh",
    )(*flat)


def spread_tokens(states, labels, lengths, segments, destinations, gain, head_in, head_out):
    row_count, slot_span, width = states.shape
    tokens_most = row_count * slot_span
    f = lax.axis_index("fsdp")
    r = lax.axis_index("rep")
    z = f // 2
    c = f % 2
    inner = (z == 1) | (z == 2)
    units = head_in.shape[1] // 4
    wide = head_in.shape[0]
    flat_states = states.reshape(-1, width)

    row_ids = jnp.arange(row_count)
    ends_row = jnp.sum(jnp.where(row_ids[:, None] >= row_ids[None, :], lengths[None, :], 0), axis=1)
    place = jnp.where(
        jnp.arange(slot_span)[None, :] < lengths[:, None],
        (ends_row - lengths)[:, None] + jnp.arange(slot_span)[None, :],
        -1,
    ).reshape(-1)

    def compacted(first, count):
        spots = first + jnp.arange(count, dtype=jnp.int32)
        picks = (place[None, :] == spots[:, None]).astype(jnp.bfloat16)
        tokens = jnp.dot(picks, flat_states, preferred_element_type=jnp.float32)
        return normalize(tokens.astype(jnp.bfloat16), gain)

    def gathered(first, count, weights=None, facts=None):
        quarter = count // 4
        mine = compacted(first + r * quarter, quarter)
        parts, weights, facts = around(mine, compacted(first, count), inner, weights, facts)
        plain = (first + jnp.arange(count))[None, :]
        moved = jnp.concatenate([first + (r ^ j) * quarter + jnp.arange(quarter) for j in range(4)])[None, :]
        spots = jnp.stack([plain, moved, moved, moved]).astype(jnp.float32)
        return parts, spots, weights, facts

    counts = jnp.sum(member_of(segments, lengths), axis=1)
    target = destinations[:, 0]
    slot_of = target * (8 * CAP) + f * CAP + rank_of(target)
    facts = jnp.concatenate(
        [counts.reshape(-1), labels.astype(jnp.float32).reshape(-1), slot_of.astype(jnp.float32)]
    )
    facts = jnp.pad(facts, (0, 384 - facts.shape[0]))
    head_t = jnp.transpose(head_in).reshape(4, units, wide)
    main_parts, main_spots, own_head, facts_all = gathered(0, LOCAL, head_t, facts)
    steps = row_count * STEPS
    counts_all = facts_all[:, :steps]
    labels_all = facts_all[:, steps : 2 * steps]
    slots_all = facts_all[:, 2 * steps : 2 * steps + row_count].reshape(-1)
    upto = jnp.arange(steps)[:, None] >= jnp.arange(steps)[None, :]
    ends_all = jnp.sum(jnp.where(upto[None], counts_all[:, None, :], 0.0), axis=2)
    lows_all = ends_all - counts_all
    overflow = jnp.max(ends_all[:, steps - 1]) > LOCAL

    sources = [z, z ^ 1, jnp.where(z < 2, 2, 1), jnp.where(z < 2, 3, 0)]
    takes = [jnp.arange(8) == source * 2 + c for source in sources]

    def of_chips(values):
        return jnp.stack([jnp.sum(jnp.where(take[:, None], values, 0.0), axis=0) for take in takes])

    bounds = jnp.stack([of_chips(lows_all), of_chips(ends_all)], axis=2)
    labels_here = of_chips(labels_all)
    live_here = jnp.minimum(of_chips(counts_all), 1.0)

    def of_lines(chip_sums):
        return sum(jnp.where(take[:, None], chip_sums[i][None, :], 0.0) for i, take in enumerate(takes))

    mate_head = core_swap(own_head)
    share = lax.dynamic_slice_in_dim(head_out, z * units, units)[:, None]
    rate = 0.5 / math.sqrt(row_count * 8 * slot_span)
    blocks_at = [(j * 2 + core) * wide for core in (c, 1 - c) for j in range(4)]
    offsets = jnp.stack(blocks_at).astype(jnp.int32)

    def scored(parts, spots):
        return first_scores(parts, own_head, mate_head, share, spots, bounds, offsets)

    def pre_grad_of(pre, spots, step_error):
        errors = []
        for i in range(4):
            inside = (spots[i] >= bounds[i, :, 0:1]) & (spots[i] < bounds[i, :, 1:2])
            errors.append(jnp.sum(jnp.where(inside, step_error[i][:, None], 0.0), axis=0))
        return (jnp.concatenate(errors)[None, :] * share * silu_slope(pre)).astype(jnp.bfloat16)

    def rest_of(batches):
        chip_sums = sum(sums[:, :, 0] for _, (_, sums, _, _) in batches)
        step_score = of_chips(sum_over_chips(of_lines(chip_sums)))
        step_error = live_here * (step_score - labels_here)
        terms = []
        for spots, (pre, _, kept, given) in batches:
            pre_grad = pre_grad_of(pre, spots, step_error)
            terms += [(pre_grad, kept), (core_swap(pre_grad), core_swap(given))]
        grads, own_fresh = grads_and_fresh(own_head, terms, rate)
        returned = lax.all_to_all(
            grads, "fsdp", 0, 0, axis_index_groups=[[0, 2, 4, 6], [1, 3, 5, 7]], tiled=True
        )
        mate_fresh = core_swap(own_fresh)
        fresh_sums = sum(
            fresh_scores(kept, given, own_fresh, mate_fresh, share, spots, bounds)[:, :, 0]
            for spots, (_, _, kept, given) in batches
        )
        lines = of_lines(fresh_sums)
        lines = lines + core_swap(lines)
        reward = sum_in_turn(lines).reshape(8 * row_count, STEPS)
        wanted = f * (8 * CAP) + jnp.arange(8 * CAP, dtype=jnp.int32)
        hits = slots_all[None, :] == wanted[:, None].astype(jnp.float32)
        step_rewards = jnp.sum(jnp.where(hits[:, :, None], reward[None], 0.0), axis=1)
        head_grad = jnp.transpose(returned.reshape(4 * units, wide)).astype(jnp.float32)
        return step_rewards, head_grad

    main_batch = (main_spots, scored(main_parts, main_spots))
    if LOCAL == tokens_most:
        return rest_of([main_batch])

    def with_more():
        more_parts, more_spots, _, _ = gathered(LOCAL, tokens_most - LOCAL)
        return rest_of([main_batch, (more_spots, scored(more_parts, more_spots))])

    return lax.cond(overflow, with_more, lambda: rest_of([main_batch]))


def solution(mesh):
    in_specs = (
        P("fsdp", None, None),
        P("fsdp", None),
        P("fsdp"),
        P("fsdp", None),
        P("fsdp", None),
        P(),
        P("fsdp", "rep"),
        P("rep"),
    )
    out_specs = (P("fsdp", None), P("fsdp", "rep"))

    def local(states, *rest):
        if lax.axis_size("rep") == 4 and lax.axis_size("fsdp") == 8:
            return spread_tokens(states, *rest)
        return gathered_weights(states, *rest)

    return jax.shard_map(local, mesh=mesh, in_specs=in_specs, out_specs=out_specs, check_vma=False)
```

```python
import functools
import math

import jax
import jax.numpy as jnp
from jax import lax
from jax.experimental import pallas as pl
from jax.experimental.pallas import tpu as pltpu
from jax.sharding import PartitionSpec as P

CAP = 2
STEPS = 8
LOCAL = 384
VMEM_BYTES = 52 * 1024 * 1024


def silu_slope(pre_act):
    sigma = jax.nn.sigmoid(pre_act)
    return sigma * (1.0 + pre_act * (1.0 - sigma))


def normalize(tokens_flat, gain):
    wide = tokens_flat.astype(jnp.float32)
    meansq = jnp.mean(wide * wide, axis=1, keepdims=True)
    return (wide * lax.rsqrt(meansq + 1e-06) * gain[None, :]).astype(jnp.bfloat16)


def member_of(segments, lengths):
    positions = jnp.arange(segments.shape[1], dtype=jnp.int32)
    valid = (positions[None, :] < lengths[:, None]).astype(jnp.float32)
    step_ids = jnp.arange(STEPS, dtype=jnp.int32)
    return (segments[:, :, None] == step_ids[None, None, :]).astype(jnp.float32) * valid[:, :, None]


def rank_of(target):
    order = jnp.arange(target.shape[0], dtype=jnp.int32)
    earlier = (target[:, None] == target[None, :]) & (order[None, :] < order[:, None])
    return jnp.sum(earlier.astype(jnp.int32), axis=1)


def gathered_weights(states, labels, lengths, segments, destinations, gain, head_in, head_out):
    row_count, slot_span, feature_width = states.shape
    trainers = lax.axis_size("fsdp")
    slot_total = trainers * CAP
    normed = normalize(states.reshape(-1, feature_width), gain)
    member = member_of(segments, lengths)
    live = jnp.max(member, axis=1)

    def scored(weights):
        pre_act = jnp.dot(normed, weights, preferred_element_type=jnp.float32)
        partial = jnp.sum(jax.nn.silu(pre_act) * head_out[None, :], axis=1)
        return pre_act, lax.psum(partial, "rep").reshape(row_count, slot_span)

    pre_act, score = scored(lax.all_gather(head_in, "fsdp", axis=0, tiled=True))
    step_score = jnp.einsum("rs,rsk->rk", score, member, precision=lax.Precision.HIGHEST)
    step_error = live * (step_score - labels.astype(jnp.float32))
    token_error = jnp.einsum("rk,rsk->rs", step_error, member, precision=lax.Precision.HIGHEST).reshape(-1)
    pre_grad = (token_error[:, None] * head_out[None, :] * silu_slope(pre_act)).astype(jnp.bfloat16)
    rate = 0.5 / math.sqrt(row_count * trainers * slot_span)
    head_grad = lax.psum_scatter(
        lax.dot_general(normed, pre_grad, (((0,), (0,)), ((), ())), preferred_element_type=jnp.float32),
        "fsdp",
        scatter_dimension=0,
        tiled=True,
    )
    fresh = (head_in.astype(jnp.float32) - rate * head_grad).astype(jnp.bfloat16)
    _, fresh_score = scored(lax.all_gather(fresh, "fsdp", axis=0, tiled=True))
    reward = jnp.einsum("rs,rsk->rk", fresh_score, member, precision=lax.Precision.HIGHEST)
    target = destinations[:, 0]
    slot = target * CAP + rank_of(target)
    placing = (slot[None, :] == jnp.arange(slot_total, dtype=jnp.int32)[:, None]).astype(jnp.float32)
    placed = jnp.dot(placing, reward, precision=lax.Precision.HIGHEST)
    return lax.all_to_all(placed, "fsdp", split_axis=0, concat_axis=0, tiled=True), head_grad


X_MATE = [(r, r ^ 1) for r in range(4)]
Y_MATE = [(r, r ^ 2) for r in range(4)]
XY_MATE = [(r, r ^ 3) for r in range(4)]
CORE_MATE = [(f, f ^ 1) for f in range(8)]
Z1_MATE = [(f, f ^ 2) for f in range(8)]
Z2_MATE = [(f, f ^ 4) for f in range(8)]
Z3_MATE = [(f, f ^ 6) for f in range(8)]
INNER = [(f, f ^ 6) for f in (2, 3, 4, 5)]
OUTWARD = [(f, f ^ 2) for f in (2, 3, 4, 5)]


def sum_over_chips(values):
    values = (values + lax.ppermute(values, "rep", X_MATE)) + (
        lax.ppermute(values, "rep", Y_MATE) + lax.ppermute(values, "rep", XY_MATE)
    )
    return (values + lax.ppermute(values, "fsdp", Z1_MATE)) + (
        lax.ppermute(values, "fsdp", Z2_MATE) + lax.ppermute(values, "fsdp", Z3_MATE)
    )


def core_swap(values):
    return lax.ppermute(values, "fsdp", CORE_MATE)


def sum_in_turn(values):
    for axis, pairs in (("rep", X_MATE), ("rep", Y_MATE), ("fsdp", Z1_MATE), ("fsdp", Z2_MATE)):
        values = values + lax.ppermute(values, axis, pairs)
    return values


def gather_small(values):
    copies = jnp.broadcast_to(values[None], (8,) + values.shape)
    return lax.all_to_all(copies, "fsdp", split_axis=0, concat_axis=0, tiled=True)


def around(part, own, inner, weights=None, facts=None):
    half = part.shape[0] // 32 * 16
    together = lax.optimization_barrier

    def along(values, pairs):
        return lax.ppermute(values, "fsdp", pairs)

    def x_of(values):
        return lax.ppermute(values, "rep", X_MATE)

    def y_of(values):
        return lax.ppermute(values, "rep", Y_MATE)

    a, b_in = together((along(part, Z1_MATE), along(part, INNER)))
    own, a = together((own, a))
    second = (x_of(a), y_of(a), along(b_in, OUTWARD), along(a, INNER))
    if facts is not None:
        facts = gather_small(facts)
        second, facts = together((second, facts))
    ax, ay, b_out, c_in = together(second)
    b = jnp.where(inner, b_in, b_out)
    c_out = along(c_in, OUTWARD)
    a_low, a_high, bx, by = together((y_of(ax[:half]), x_of(ay[half:]), x_of(b), y_of(b)))
    c_out, bx = together((c_out, bx))
    if weights is not None:
        weights, c_out = together((weights, c_out))
        weights = lax.all_to_all(
            weights, "fsdp", 0, 0, axis_index_groups=[[0, 2, 4, 6], [1, 3, 5, 7]], tiled=True
        )
    c = jnp.where(inner, c_in, c_out)
    fourth = (y_of(bx[:half]), x_of(by[half:]), x_of(c), y_of(c))
    if weights is not None:
        fourth, weights = together((fourth, weights))
    b_low, b_high, cx, cy = together(fourth)
    c_low, c_high = y_of(cx[:half]), x_of(cy[half:])
    parts = [own, a, ax, ay, a_low, a_high, b, bx, by, b_low, b_high, c, cx, cy, c_low, c_high]
    return parts, weights, facts


def step_sums(pre, share, spots, bounds_ref, sums_ref, first):
    score = jnp.sum(pre * jax.nn.sigmoid(pre) * share, axis=0, keepdims=True)
    span = spots.shape[2]
    for at in range(2):
        chip = first + at
        here = spots[at]
        low = bounds_ref[chip, :, 0:1]
        high = bounds_ref[chip, :, 1:2]
        inside = (here >= low) & (here < high)
        sums = jnp.sum(jnp.where(inside, score[:, at * span : (at + 1) * span], 0.0), axis=1, keepdims=True)
        sums_ref[chip] = jnp.broadcast_to(sums, sums_ref.shape[1:])


def first_kernel(offsets_ref, *refs, sizes, blocks, half, carried):
    count = len(sizes)
    parts = refs[:count]
    own_w, mate_w, share_ref, spots_ref, bounds_ref = refs[count : count + 5]
    outs = refs[count + 5 + carried :]
    sums_ref, pre_ref, kept_ref, given_ref, x_s, w_s, acc_s, in_sem, w_sem, out_sem = outs
    wide = own_w.shape[2]
    tile, width = x_s.shape
    depth = width // blocks
    copies = []
    at = 0
    for index, size in enumerate(sizes):
        copies.append(pltpu.make_async_copy(parts[index], x_s.at[pl.ds(at, size)], in_sem.at[index]))
        at += size
    for core, source in enumerate((own_w, mate_w)):
        for j in range(4):
            where = pl.ds(pl.multiple_of(offsets_ref[core * 4 + j], 128), wide)
            copies.append(pltpu.make_async_copy(source.at[j], w_s.at[:, where], w_sem.at[core * 4 + j]))
    for copy in copies:
        copy.start()
    acc_s[...] = jnp.zeros_like(acc_s)
    for copy in copies:
        copy.wait()
    rows = pl.ds(half * tile, tile)
    out_copies = []
    for core, dest in enumerate((kept_ref, given_ref)):
        for j in range(4):
            where = pl.ds(pl.multiple_of(offsets_ref[core * 4 + j], 128), wide)
            out_copies.append(
                pltpu.make_async_copy(x_s.at[:, where], dest.at[j, rows], out_sem.at[core * 4 + j])
            )
            out_copies[-1].start()

    @pl.loop(0, blocks)
    def _(k):
        where = pl.ds(pl.multiple_of(k * depth, 128), depth)
        acc_s[...] += lax.dot_general(
            w_s[:, where], x_s[:, where], (((1,), (1,)), ((), ())), preferred_element_type=jnp.float32
        )

    out_copies.append(pltpu.make_async_copy(acc_s, pre_ref.at[:, rows], out_sem.at[8]))
    out_copies[-1].start()
    step_sums(acc_s[...], share_ref[...], spots_ref[...], bounds_ref, sums_ref, 0)
    for copy in out_copies:
        copy.wait()


def first_scores(parts, own_w, mate_w, share, spots, bounds, offsets, half, carried=()):
    sizes = tuple(part.shape[0] for part in parts)
    tile = sum(sizes)
    width = parts[0].shape[1]
    units, wide = own_w.shape[1:]
    anywhere = pl.BlockSpec(memory_space=pl.ANY)
    vmem = pl.BlockSpec(memory_space=pltpu.VMEM)
    both = slice(half * 2, half * 2 + 2)
    first_carried = 1 + len(parts) + 5
    return pl.pallas_call(
        functools.partial(first_kernel, sizes=sizes, blocks=5, half=half, carried=len(carried)),
        out_shape=(
            jax.ShapeDtypeStruct((2, bounds.shape[1], 128), jnp.float32),
            jax.ShapeDtypeStruct((units, 2 * tile), jnp.float32),
            jax.ShapeDtypeStruct((4, 2 * tile, wide), jnp.bfloat16),
            jax.ShapeDtypeStruct((4, 2 * tile, wide), jnp.bfloat16),
        ),
        in_specs=[pl.BlockSpec(memory_space=pltpu.SMEM)]
        + [anywhere] * (len(parts) + 2)
        + [vmem] * 3
        + [anywhere] * len(carried),
        out_specs=(vmem, anywhere, anywhere, anywhere),
        input_output_aliases={first_carried + i: 1 + i for i in range(len(carried))},
        scratch_shapes=[
            pltpu.VMEM((tile, width), jnp.bfloat16),
            pltpu.VMEM((units, width), jnp.bfloat16),
            pltpu.VMEM((units, tile), jnp.float32),
            pltpu.SemaphoreType.DMA((len(parts),)),
            pltpu.SemaphoreType.DMA((8,)),
            pltpu.SemaphoreType.DMA((9,)),
        ],
        compiler_params=pltpu.CompilerParams(vmem_limit_bytes=VMEM_BYTES),
        cost_estimate=pl.CostEstimate(
            flops=2 * units * width * tile, bytes_accessed=4 * tile * width, transcendentals=units * tile
        ),
        name="first_scores",
    )(offsets, *parts, own_w, mate_w, share, spots[both], bounds[both], *carried)


def fresh_kernel(kept_ref, given_ref, own_w, mate_w, share_ref, spots_ref, bounds_ref, sums_ref, acc_s):
    half = pl.program_id(0)
    k = pl.program_id(1)
    contract = (((1,), (1,)), ((), ()))
    term = lax.dot_general(own_w[0], kept_ref[0], contract, preferred_element_type=jnp.float32)
    term = term + lax.dot_general(mate_w[0], given_ref[0], contract, preferred_element_type=jnp.float32)

    @pl.when(k == 0)
    def _():
        acc_s[...] = term

    @pl.when(k > 0)
    def _():
        acc_s[...] += term

    @pl.when(k == 3)
    def _():
        step_sums(acc_s[...], share_ref[...], spots_ref[...], bounds_ref, sums_ref, 0)


def fresh_scores(kept, given, own_w, mate_w, share, spots, bounds):
    total, wide = kept.shape[1:]
    units = own_w.shape[1]
    steps = bounds.shape[1]
    tile = total // 2
    tokens = pl.BlockSpec((1, tile, wide), lambda h, k: (k, h, 0))
    weights = pl.BlockSpec((1, units, wide), lambda h, k: (k, 0, 0))
    return pl.pallas_call(
        fresh_kernel,
        grid=(2, 4),
        out_shape=jax.ShapeDtypeStruct((4, steps, 128), jnp.float32),
        in_specs=[
            tokens,
            tokens,
            weights,
            weights,
            pl.BlockSpec((units, 1), lambda h, k: (0, 0)),
            pl.BlockSpec((2,) + spots.shape[1:], lambda h, k: (h, 0, 0)),
            pl.BlockSpec((2, steps, 2), lambda h, k: (h, 0, 0)),
        ],
        out_specs=pl.BlockSpec((2, steps, 128), lambda h, k: (h, 0, 0)),
        scratch_shapes=[pltpu.VMEM((units, tile), jnp.float32)],
        compiler_params=pltpu.CompilerParams(vmem_limit_bytes=VMEM_BYTES),
        cost_estimate=pl.CostEstimate(
            flops=4 * units * wide * 4 * total, bytes_accessed=16 * total * wide, transcendentals=units * total
        ),
        name="fresh_scores",
    )(kept, given, own_w, mate_w, share, spots, bounds)


def grad_kernel(rate, count, *refs):
    head_ref = refs[0]
    ins = refs[1 : 1 + 2 * count]
    grad_ref, fresh_ref = refs[1 + 2 * count :]
    grad = jnp.dot(ins[0][...], ins[1][0], preferred_element_type=jnp.float32)
    for at in range(2, 2 * count, 2):
        grad = grad + jnp.dot(ins[at][...], ins[at + 1][0], preferred_element_type=jnp.float32)
    grad_ref[0] = grad.astype(grad_ref.dtype)
    fresh_ref[0] = (head_ref[0].astype(jnp.float32) - rate * grad).astype(fresh_ref.dtype)


def grads_and_fresh(head, terms, rate):
    units, wide = head.shape[1:]
    block = pl.BlockSpec((1, units, wide), lambda j: (j, 0, 0))
    specs = [block]
    flat = [head]
    work = 0
    for pre_grad, tokens in terms:
        specs.append(pl.BlockSpec(pre_grad.shape, lambda j: (0, 0)))
        specs.append(pl.BlockSpec((1,) + tokens.shape[1:], lambda j: (j, 0, 0)))
        flat += [pre_grad, tokens]
        work += tokens.size
    return pl.pallas_call(
        functools.partial(grad_kernel, rate, len(terms)),
        grid=(4,),
        out_shape=(jax.ShapeDtypeStruct(head.shape, jnp.bfloat16),) * 2,
        in_specs=specs,
        out_specs=(block, block),
        compiler_params=pltpu.CompilerParams(vmem_limit_bytes=VMEM_BYTES),
        cost_estimate=pl.CostEstimate(flops=2 * units * work, bytes_accessed=2 * work, transcendentals=0),
        name="grads_and_fresh",
    )(*flat)


def spread_tokens(states, labels, lengths, segments, destinations, gain, head_in, head_out):
    row_count, slot_span, width = states.shape
    tokens_most = row_count * slot_span
    f = lax.axis_index("fsdp")
    r = lax.axis_index("rep")
    z = f // 2
    c = f % 2
    inner = (z == 1) | (z == 2)
    units = head_in.shape[1] // 4
    wide = head_in.shape[0]
    flat_states = states.reshape(-1, width)

    row_ids = jnp.arange(row_count)
    ends_row = jnp.sum(jnp.where(row_ids[:, None] >= row_ids[None, :], lengths[None, :], 0), axis=1)
    place = jnp.where(
        jnp.arange(slot_span)[None, :] < lengths[:, None],
        (ends_row - lengths)[:, None] + jnp.arange(slot_span)[None, :],
        -1,
    ).reshape(-1)

    def compacted(first, count):
        spots = first + jnp.arange(count, dtype=jnp.int32)
        picks = (place[None, :] == spots[:, None]).astype(jnp.bfloat16)
        tokens = jnp.dot(picks, flat_states, preferred_element_type=jnp.float32)
        return normalize(tokens.astype(jnp.bfloat16), gain)

    def gathered(first, count, weights=None, facts=None):
        quarter = count // 4
        mine = compacted(first + r * quarter, quarter)
        parts, weights, facts = around(mine, compacted(first, count), inner, weights, facts)
        plain = (first + jnp.arange(count))[None, :]
        moved = jnp.concatenate([first + (r ^ j) * quarter + jnp.arange(quarter) for j in range(4)])[None, :]
        spots = jnp.stack([plain, moved, moved, moved]).astype(jnp.float32)
        return parts, spots, weights, facts

    counts = jnp.sum(member_of(segments, lengths), axis=1)
    target = destinations[:, 0]
    slot_of = target * (8 * CAP) + f * CAP + rank_of(target)
    facts = jnp.concatenate(
        [counts.reshape(-1), labels.astype(jnp.float32).reshape(-1), slot_of.astype(jnp.float32)]
    )
    facts = jnp.pad(facts, (0, 384 - facts.shape[0]))
    head_t = jnp.transpose(head_in).reshape(4, units, wide)
    main_parts, main_spots, own_head, facts_all = gathered(0, LOCAL, head_t, facts)
    steps = row_count * STEPS
    counts_all = facts_all[:, :steps]
    labels_all = facts_all[:, steps : 2 * steps]
    slots_all = facts_all[:, 2 * steps : 2 * steps + row_count].reshape(-1)
    upto = jnp.arange(steps)[:, None] >= jnp.arange(steps)[None, :]
    ends_all = jnp.sum(jnp.where(upto[None], counts_all[:, None, :], 0.0), axis=2)
    lows_all = ends_all - counts_all
    overflow = jnp.max(ends_all[:, steps - 1]) > LOCAL

    sources = [z, z ^ 1, jnp.where(z < 2, 2, 1), jnp.where(z < 2, 3, 0)]
    takes = [jnp.arange(8) == source * 2 + c for source in sources]

    def of_chips(values):
        return jnp.stack([jnp.sum(jnp.where(take[:, None], values, 0.0), axis=0) for take in takes])

    bounds = jnp.stack([of_chips(lows_all), of_chips(ends_all)], axis=2)
    labels_here = of_chips(labels_all)
    live_here = jnp.minimum(of_chips(counts_all), 1.0)

    def of_lines(chip_sums):
        return sum(jnp.where(take[:, None], chip_sums[i][None, :], 0.0) for i, take in enumerate(takes))

    mate_head = core_swap(own_head)
    share = lax.dynamic_slice_in_dim(head_out, z * units, units)[:, None]
    rate = 0.5 / math.sqrt(row_count * 8 * slot_span)
    blocks_at = [(j * 2 + core) * wide for core in (c, 1 - c) for j in range(4)]
    offsets = jnp.stack(blocks_at).astype(jnp.int32)

    def scored(parts, spots):
        facts_of = (own_head, mate_head, share, spots, bounds, offsets)
        low_sums, *carried = first_scores(parts[:6], *facts_of, 0)
        high_sums, *carried = first_scores(parts[6:], *facts_of, 1, carried)
        return (jnp.concatenate([low_sums, high_sums]), *carried)

    def pre_grad_of(pre, spots, step_error):
        errors = []
        for i in range(4):
            inside = (spots[i] >= bounds[i, :, 0:1]) & (spots[i] < bounds[i, :, 1:2])
            errors.append(jnp.sum(jnp.where(inside, step_error[i][:, None], 0.0), axis=0))
        return (jnp.concatenate(errors)[None, :] * share * silu_slope(pre)).astype(jnp.bfloat16)

    def rest_of(batches):
        chip_sums = sum(sums[:, :, 0] for _, (sums, _, _, _) in batches)
        step_score = of_chips(sum_over_chips(of_lines(chip_sums)))
        step_error = live_here * (step_score - labels_here)
        terms = []
        for spots, (_, pre, kept, given) in batches:
            pre_grad = pre_grad_of(pre, spots, step_error)
            terms += [(pre_grad, kept), (core_swap(pre_grad), core_swap(given))]
        grads, own_fresh = grads_and_fresh(own_head, terms, rate)
        returned = lax.all_to_all(
            grads, "fsdp", 0, 0, axis_index_groups=[[0, 2, 4, 6], [1, 3, 5, 7]], tiled=True
        )
        mate_fresh = core_swap(own_fresh)
        fresh_sums = sum(
            fresh_scores(kept, given, own_fresh, mate_fresh, share, spots, bounds)[:, :, 0]
            for spots, (_, _, kept, given) in batches
        )
        lines = of_lines(fresh_sums)
        lines = lines + core_swap(lines)
        reward = sum_in_turn(lines).reshape(8 * row_count, STEPS)
        wanted = f * (8 * CAP) + jnp.arange(8 * CAP, dtype=jnp.int32)
        hits = slots_all[None, :] == wanted[:, None].astype(jnp.float32)
        step_rewards = jnp.sum(jnp.where(hits[:, :, None], reward[None], 0.0), axis=1)
        head_grad = jnp.transpose(returned.reshape(4 * units, wide)).astype(jnp.float32)
        return step_rewards, head_grad

    main_batch = (main_spots, scored(main_parts, main_spots))
    if LOCAL == tokens_most:
        return rest_of([main_batch])

    def with_more():
        more_parts, more_spots, _, _ = gathered(LOCAL, tokens_most - LOCAL)
        return rest_of([main_batch, (more_spots, scored(more_parts, more_spots))])

    return lax.cond(overflow, with_more, lambda: rest_of([main_batch]))


def solution(mesh):
    in_specs = (
        P("fsdp", None, None),
        P("fsdp", None),
        P("fsdp"),
        P("fsdp", None),
        P("fsdp", None),
        P(),
        P("fsdp", "rep"),
        P("rep"),
    )
    out_specs = (P("fsdp", None), P("fsdp", "rep"))

    def local(states, *rest):
        if lax.axis_size("rep") == 4 and lax.axis_size("fsdp") == 8:
            return spread_tokens(states, *rest)
        return gathered_weights(states, *rest)

    return jax.shard_map(local, mesh=mesh, in_specs=in_specs, out_specs=out_specs, check_vma=False)
```

```python
import functools
import math

import jax
import jax.numpy as jnp
from jax import lax
from jax.experimental import pallas as pl
from jax.experimental.pallas import tpu as pltpu
from jax.sharding import PartitionSpec as P

CAP = 2
STEPS = 8
LOCAL = 384
VMEM_BYTES = 52 * 1024 * 1024


def silu_slope(pre_act):
    sigma = jax.nn.sigmoid(pre_act)
    return sigma * (1.0 + pre_act * (1.0 - sigma))


def normalize(tokens_flat, gain):
    wide = tokens_flat.astype(jnp.float32)
    meansq = jnp.mean(wide * wide, axis=1, keepdims=True)
    return (wide * lax.rsqrt(meansq + 1e-06) * gain[None, :]).astype(jnp.bfloat16)


def member_of(segments, lengths):
    positions = jnp.arange(segments.shape[1], dtype=jnp.int32)
    valid = (positions[None, :] < lengths[:, None]).astype(jnp.float32)
    step_ids = jnp.arange(STEPS, dtype=jnp.int32)
    return (segments[:, :, None] == step_ids[None, None, :]).astype(jnp.float32) * valid[:, :, None]


def rank_of(target):
    order = jnp.arange(target.shape[0], dtype=jnp.int32)
    earlier = (target[:, None] == target[None, :]) & (order[None, :] < order[:, None])
    return jnp.sum(earlier.astype(jnp.int32), axis=1)


def gathered_weights(states, labels, lengths, segments, destinations, gain, head_in, head_out):
    row_count, slot_span, feature_width = states.shape
    trainers = lax.axis_size("fsdp")
    slot_total = trainers * CAP
    normed = normalize(states.reshape(-1, feature_width), gain)
    member = member_of(segments, lengths)
    live = jnp.max(member, axis=1)

    def scored(weights):
        pre_act = jnp.dot(normed, weights, preferred_element_type=jnp.float32)
        partial = jnp.sum(jax.nn.silu(pre_act) * head_out[None, :], axis=1)
        return pre_act, lax.psum(partial, "rep").reshape(row_count, slot_span)

    pre_act, score = scored(lax.all_gather(head_in, "fsdp", axis=0, tiled=True))
    step_score = jnp.einsum("rs,rsk->rk", score, member, precision=lax.Precision.HIGHEST)
    step_error = live * (step_score - labels.astype(jnp.float32))
    token_error = jnp.einsum("rk,rsk->rs", step_error, member, precision=lax.Precision.HIGHEST).reshape(-1)
    pre_grad = (token_error[:, None] * head_out[None, :] * silu_slope(pre_act)).astype(jnp.bfloat16)
    rate = 0.5 / math.sqrt(row_count * trainers * slot_span)
    head_grad = lax.psum_scatter(
        lax.dot_general(normed, pre_grad, (((0,), (0,)), ((), ())), preferred_element_type=jnp.float32),
        "fsdp",
        scatter_dimension=0,
        tiled=True,
    )
    fresh = (head_in.astype(jnp.float32) - rate * head_grad).astype(jnp.bfloat16)
    _, fresh_score = scored(lax.all_gather(fresh, "fsdp", axis=0, tiled=True))
    reward = jnp.einsum("rs,rsk->rk", fresh_score, member, precision=lax.Precision.HIGHEST)
    target = destinations[:, 0]
    slot = target * CAP + rank_of(target)
    placing = (slot[None, :] == jnp.arange(slot_total, dtype=jnp.int32)[:, None]).astype(jnp.float32)
    placed = jnp.dot(placing, reward, precision=lax.Precision.HIGHEST)
    return lax.all_to_all(placed, "fsdp", split_axis=0, concat_axis=0, tiled=True), head_grad


X_MATE = [(r, r ^ 1) for r in range(4)]
Y_MATE = [(r, r ^ 2) for r in range(4)]
XY_MATE = [(r, r ^ 3) for r in range(4)]
CORE_MATE = [(f, f ^ 1) for f in range(8)]
Z1_MATE = [(f, f ^ 2) for f in range(8)]
Z2_MATE = [(f, f ^ 4) for f in range(8)]
Z3_MATE = [(f, f ^ 6) for f in range(8)]
INNER = [(f, f ^ 6) for f in (2, 3, 4, 5)]
OUTWARD = [(f, f ^ 2) for f in (2, 3, 4, 5)]


def sum_over_chips(values):
    values = (values + lax.ppermute(values, "rep", X_MATE)) + (
        lax.ppermute(values, "rep", Y_MATE) + lax.ppermute(values, "rep", XY_MATE)
    )
    return (values + lax.ppermute(values, "fsdp", Z1_MATE)) + (
        lax.ppermute(values, "fsdp", Z2_MATE) + lax.ppermute(values, "fsdp", Z3_MATE)
    )


def core_swap(values):
    return lax.ppermute(values, "fsdp", CORE_MATE)


def sum_in_turn(values):
    for axis, pairs in (("rep", X_MATE), ("rep", Y_MATE), ("fsdp", Z1_MATE), ("fsdp", Z2_MATE)):
        values = values + lax.ppermute(values, axis, pairs)
    return values


def gather_small(values):
    copies = jnp.broadcast_to(values[None], (8,) + values.shape)
    return lax.all_to_all(copies, "fsdp", split_axis=0, concat_axis=0, tiled=True)


def around(part, own, inner, weights=None, facts=None):
    half = part.shape[0] // 32 * 16
    together = lax.optimization_barrier

    def along(values, pairs):
        return lax.ppermute(values, "fsdp", pairs)

    def x_of(values):
        return lax.ppermute(values, "rep", X_MATE)

    def y_of(values):
        return lax.ppermute(values, "rep", Y_MATE)

    a, b_in = together((along(part, Z1_MATE), along(part, INNER)))
    own, a = together((own, a))
    second = (x_of(a), y_of(a), along(b_in, OUTWARD), along(a, INNER))
    if facts is not None:
        facts = gather_small(facts)
        second, facts = together((second, facts))
    ax, ay, b_out, c_in = together(second)
    b = jnp.where(inner, b_in, b_out)
    c_out = along(c_in, OUTWARD)
    if weights is not None:
        weights, ax = together((weights, ax))
        weights = lax.all_to_all(
            jnp.transpose(weights).reshape(4, -1, weights.shape[0]),
            "fsdp",
            0,
            0,
            axis_index_groups=[[0, 2, 4, 6], [1, 3, 5, 7]],
            tiled=True,
        )
    a_low, a_high, bx, by = together((y_of(ax[:half]), x_of(ay[half:]), x_of(b), y_of(b)))
    c_out, bx = together((c_out, bx))
    c = jnp.where(inner, c_in, c_out)
    fourth = (y_of(bx[:half]), x_of(by[half:]), x_of(c), y_of(c))
    if weights is not None:
        fourth, weights = together((fourth, weights))
    b_low, b_high, cx, cy = together(fourth)
    c_low, c_high = y_of(cx[:half]), x_of(cy[half:])
    parts = [own, a, ax, ay, a_low, a_high, b, bx, by, b_low, b_high, c, cx, cy, c_low, c_high]
    return parts, weights, facts


def step_sums(pre, share, spots, bounds_ref, sums_ref):
    score = jnp.sum(pre * jax.nn.sigmoid(pre) * share, axis=0, keepdims=True)
    span = spots.shape[2]
    for at in range(spots.shape[0]):
        here = spots[at]
        low = bounds_ref[at, :, 0:1]
        high = bounds_ref[at, :, 1:2]
        inside = (here >= low) & (here < high)
        sums = jnp.sum(jnp.where(inside, score[:, at * span : (at + 1) * span], 0.0), axis=1, keepdims=True)
        sums_ref[at] = jnp.broadcast_to(sums, sums_ref.shape[1:])


def first_kernel(offsets_ref, *refs, sizes, blocks, first, carried):
    count = len(sizes)
    parts = refs[:count]
    own_w, mate_w, share_ref, spots_ref, bounds_ref = refs[count : count + 5]
    outs = refs[count + 5 + carried :]
    sums_ref, pre_ref, kept_ref, given_ref, x_s, w_s, acc_s, in_sem, w_sem, out_sem = outs
    wide = own_w.shape[2]
    tile, width = x_s.shape
    depth = width // blocks
    copies = []
    at = 0
    for index, size in enumerate(sizes):
        copies.append(pltpu.make_async_copy(parts[index], x_s.at[pl.ds(at, size)], in_sem.at[index]))
        at += size
    for core, source in enumerate((own_w, mate_w)):
        for j in range(4):
            where = pl.ds(pl.multiple_of(offsets_ref[core * 4 + j], 128), wide)
            copies.append(pltpu.make_async_copy(source.at[j], w_s.at[:, where], w_sem.at[core * 4 + j]))
    for copy in copies:
        copy.start()
    acc_s[...] = jnp.zeros_like(acc_s)
    for copy in copies:
        copy.wait()
    rows = pl.ds(first, tile)
    out_copies = []
    for core, dest in enumerate((kept_ref, given_ref)):
        for j in range(4):
            where = pl.ds(pl.multiple_of(offsets_ref[core * 4 + j], 128), wide)
            out_copies.append(
                pltpu.make_async_copy(x_s.at[:, where], dest.at[j, rows], out_sem.at[core * 4 + j])
            )
            out_copies[-1].start()

    @pl.loop(0, blocks)
    def _(k):
        where = pl.ds(pl.multiple_of(k * depth, 128), depth)
        acc_s[...] += lax.dot_general(
            w_s[:, where], x_s[:, where], (((1,), (1,)), ((), ())), preferred_element_type=jnp.float32
        )

    out_copies.append(pltpu.make_async_copy(acc_s, pre_ref.at[:, rows], out_sem.at[8]))
    out_copies[-1].start()
    step_sums(acc_s[...], share_ref[...], spots_ref[...], bounds_ref, sums_ref)
    for copy in out_copies:
        copy.wait()


def first_scores(parts, own_w, mate_w, share, spots, bounds, offsets, first, chips, carried=()):
    sizes = tuple(part.shape[0] for part in parts)
    tile = sum(sizes)
    width = parts[0].shape[1]
    units, wide = own_w.shape[1:]
    anywhere = pl.BlockSpec(memory_space=pl.ANY)
    vmem = pl.BlockSpec(memory_space=pltpu.VMEM)
    here = slice(first, first + chips)
    total = tile // chips * 4
    first_carried = 1 + len(parts) + 5
    return pl.pallas_call(
        functools.partial(first_kernel, sizes=sizes, blocks=5, first=first * (tile // chips), carried=len(carried)),
        out_shape=(
            jax.ShapeDtypeStruct((chips, bounds.shape[1], 128), jnp.float32),
            jax.ShapeDtypeStruct((units, total), jnp.float32),
            jax.ShapeDtypeStruct((4, total, wide), jnp.bfloat16),
            jax.ShapeDtypeStruct((4, total, wide), jnp.bfloat16),
        ),
        in_specs=[pl.BlockSpec(memory_space=pltpu.SMEM)]
        + [anywhere] * (len(parts) + 2)
        + [vmem] * 3
        + [anywhere] * len(carried),
        out_specs=(vmem, anywhere, anywhere, anywhere),
        input_output_aliases={first_carried + i: 1 + i for i in range(len(carried))},
        scratch_shapes=[
            pltpu.VMEM((tile, width), jnp.bfloat16),
            pltpu.VMEM((units, width), jnp.bfloat16),
            pltpu.VMEM((units, tile), jnp.float32),
            pltpu.SemaphoreType.DMA((len(parts),)),
            pltpu.SemaphoreType.DMA((8,)),
            pltpu.SemaphoreType.DMA((9,)),
        ],
        compiler_params=pltpu.CompilerParams(vmem_limit_bytes=VMEM_BYTES),
        cost_estimate=pl.CostEstimate(
            flops=2 * units * width * tile, bytes_accessed=4 * tile * width, transcendentals=units * tile
        ),
        name="first_scores",
    )(offsets, *parts, own_w, mate_w, share, spots[here], bounds[here], *carried)


def fresh_kernel(kept_ref, given_ref, own_w, mate_w, share_ref, spots_ref, bounds_ref, sums_ref, acc_s):
    half = pl.program_id(0)
    k = pl.program_id(1)
    contract = (((1,), (1,)), ((), ()))
    term = lax.dot_general(own_w[0], kept_ref[0], contract, preferred_element_type=jnp.float32)
    term = term + lax.dot_general(mate_w[0], given_ref[0], contract, preferred_element_type=jnp.float32)

    @pl.when(k == 0)
    def _():
        acc_s[...] = term

    @pl.when(k > 0)
    def _():
        acc_s[...] += term

    @pl.when(k == 3)
    def _():
        step_sums(acc_s[...], share_ref[...], spots_ref[...], bounds_ref, sums_ref)


def fresh_scores(kept, given, own_w, mate_w, share, spots, bounds):
    total, wide = kept.shape[1:]
    units = own_w.shape[1]
    steps = bounds.shape[1]
    tile = total // 2
    tokens = pl.BlockSpec((1, tile, wide), lambda h, k: (k, h, 0))
    weights = pl.BlockSpec((1, units, wide), lambda h, k: (k, 0, 0))
    return pl.pallas_call(
        fresh_kernel,
        grid=(2, 4),
        out_shape=jax.ShapeDtypeStruct((4, steps, 128), jnp.float32),
        in_specs=[
            tokens,
            tokens,
            weights,
            weights,
            pl.BlockSpec((units, 1), lambda h, k: (0, 0)),
            pl.BlockSpec((2,) + spots.shape[1:], lambda h, k: (h, 0, 0)),
            pl.BlockSpec((2, steps, 2), lambda h, k: (h, 0, 0)),
        ],
        out_specs=pl.BlockSpec((2, steps, 128), lambda h, k: (h, 0, 0)),
        scratch_shapes=[pltpu.VMEM((units, tile), jnp.float32)],
        compiler_params=pltpu.CompilerParams(vmem_limit_bytes=VMEM_BYTES),
        cost_estimate=pl.CostEstimate(
            flops=4 * units * wide * 4 * total, bytes_accessed=16 * total * wide, transcendentals=units * total
        ),
        name="fresh_scores",
    )(kept, given, own_w, mate_w, share, spots, bounds)


def grad_kernel(rate, count, *refs):
    head_ref = refs[0]
    ins = refs[1 : 1 + 2 * count]
    grad_ref, fresh_ref = refs[1 + 2 * count :]
    grad = jnp.dot(ins[0][...], ins[1][0], preferred_element_type=jnp.float32)
    for at in range(2, 2 * count, 2):
        grad = grad + jnp.dot(ins[at][...], ins[at + 1][0], preferred_element_type=jnp.float32)
    grad_ref[0] = grad.astype(grad_ref.dtype)
    fresh_ref[0] = (head_ref[0].astype(jnp.float32) - rate * grad).astype(fresh_ref.dtype)


def grads_and_fresh(head, terms, rate):
    units, wide = head.shape[1:]
    block = pl.BlockSpec((1, units, wide), lambda j: (j, 0, 0))
    specs = [block]
    flat = [head]
    work = 0
    for pre_grad, tokens in terms:
        specs.append(pl.BlockSpec(pre_grad.shape, lambda j: (0, 0)))
        specs.append(pl.BlockSpec((1,) + tokens.shape[1:], lambda j: (j, 0, 0)))
        flat += [pre_grad, tokens]
        work += tokens.size
    return pl.pallas_call(
        functools.partial(grad_kernel, rate, len(terms)),
        grid=(4,),
        out_shape=(jax.ShapeDtypeStruct(head.shape, jnp.bfloat16),) * 2,
        in_specs=specs,
        out_specs=(block, block),
        compiler_params=pltpu.CompilerParams(vmem_limit_bytes=VMEM_BYTES),
        cost_estimate=pl.CostEstimate(flops=2 * units * work, bytes_accessed=2 * work, transcendentals=0),
        name="grads_and_fresh",
    )(*flat)


def spread_tokens(states, labels, lengths, segments, destinations, gain, head_in, head_out):
    row_count, slot_span, width = states.shape
    tokens_most = row_count * slot_span
    f = lax.axis_index("fsdp")
    r = lax.axis_index("rep")
    z = f // 2
    c = f % 2
    inner = (z == 1) | (z == 2)
    units = head_in.shape[1] // 4
    wide = head_in.shape[0]
    flat_states = states.reshape(-1, width)

    row_ids = jnp.arange(row_count)
    ends_row = jnp.sum(jnp.where(row_ids[:, None] >= row_ids[None, :], lengths[None, :], 0), axis=1)
    place = jnp.where(
        jnp.arange(slot_span)[None, :] < lengths[:, None],
        (ends_row - lengths)[:, None] + jnp.arange(slot_span)[None, :],
        -1,
    ).reshape(-1)

    def compacted(first, count):
        spots = first + jnp.arange(count, dtype=jnp.int32)
        picks = (place[None, :] == spots[:, None]).astype(jnp.bfloat16)
        tokens = jnp.dot(picks, flat_states, preferred_element_type=jnp.float32)
        return normalize(tokens.astype(jnp.bfloat16), gain)

    def gathered(first, count, weights=None, facts=None):
        quarter = count // 4
        mine = compacted(first + r * quarter, quarter)
        parts, weights, facts = around(mine, compacted(first, count), inner, weights, facts)
        plain = (first + jnp.arange(count))[None, :]
        moved = jnp.concatenate([first + (r ^ j) * quarter + jnp.arange(quarter) for j in range(4)])[None, :]
        spots = jnp.stack([plain, moved, moved, moved]).astype(jnp.float32)
        return parts, spots, weights, facts

    counts = jnp.sum(member_of(segments, lengths), axis=1)
    target = destinations[:, 0]
    slot_of = target * (8 * CAP) + f * CAP + rank_of(target)
    facts = jnp.concatenate(
        [counts.reshape(-1), labels.astype(jnp.float32).reshape(-1), slot_of.astype(jnp.float32)]
    )
    facts = jnp.pad(facts, (0, 384 - facts.shape[0]))
    main_parts, main_spots, own_head, facts_all = gathered(0, LOCAL, head_in, facts)
    steps = row_count * STEPS
    counts_all = facts_all[:, :steps]
    labels_all = facts_all[:, steps : 2 * steps]
    slots_all = facts_all[:, 2 * steps : 2 * steps + row_count].reshape(-1)
    upto = jnp.arange(steps)[:, None] >= jnp.arange(steps)[None, :]
    ends_all = jnp.sum(jnp.where(upto[None], counts_all[:, None, :], 0.0), axis=2)
    lows_all = ends_all - counts_all
    overflow = jnp.max(ends_all[:, steps - 1]) > LOCAL

    sources = [z, z ^ 1, jnp.where(z < 2, 2, 1), jnp.where(z < 2, 3, 0)]
    takes = [jnp.arange(8) == source * 2 + c for source in sources]

    def of_chips(values):
        return jnp.stack([jnp.sum(jnp.where(take[:, None], values, 0.0), axis=0) for take in takes])

    bounds = jnp.stack([of_chips(lows_all), of_chips(ends_all)], axis=2)
    labels_here = of_chips(labels_all)
    live_here = jnp.minimum(of_chips(counts_all), 1.0)

    def of_lines(chip_sums):
        return sum(jnp.where(take[:, None], chip_sums[i][None, :], 0.0) for i, take in enumerate(takes))

    mate_head = core_swap(own_head)
    share = lax.dynamic_slice_in_dim(head_out, z * units, units)[:, None]
    rate = 0.5 / math.sqrt(row_count * 8 * slot_span)
    blocks_at = [(j * 2 + core) * wide for core in (c, 1 - c) for j in range(4)]
    offsets = jnp.stack(blocks_at).astype(jnp.int32)

    def scored(parts, spots):
        facts_of = (own_head, mate_head, share, spots, bounds, offsets)
        near_sums, *carried = first_scores(parts[:6], *facts_of, 0, 2)
        last_sums, *carried = first_scores(parts[6:], *facts_of, 2, 2, carried)
        return (jnp.concatenate([near_sums, last_sums]), *carried)

    def pre_grad_of(pre, spots, step_error):
        errors = []
        for i in range(4):
            inside = (spots[i] >= bounds[i, :, 0:1]) & (spots[i] < bounds[i, :, 1:2])
            errors.append(jnp.sum(jnp.where(inside, step_error[i][:, None], 0.0), axis=0))
        return (jnp.concatenate(errors)[None, :] * share * silu_slope(pre)).astype(jnp.bfloat16)

    def rest_of(batches):
        chip_sums = sum(sums[:, :, 0] for _, (sums, _, _, _) in batches)
        step_score = of_chips(sum_over_chips(of_lines(chip_sums)))
        step_error = live_here * (step_score - labels_here)
        terms = []
        for spots, (_, pre, kept, given) in batches:
            pre_grad = pre_grad_of(pre, spots, step_error)
            terms += [(pre_grad, kept), (core_swap(pre_grad), core_swap(given))]
        grads, own_fresh = grads_and_fresh(own_head, terms, rate)
        returned = lax.all_to_all(
            grads, "fsdp", 0, 0, axis_index_groups=[[0, 2, 4, 6], [1, 3, 5, 7]], tiled=True
        )
        mate_fresh = core_swap(own_fresh)
        fresh_sums = sum(
            fresh_scores(kept, given, own_fresh, mate_fresh, share, spots, bounds)[:, :, 0]
            for spots, (_, _, kept, given) in batches
        )
        lines = of_lines(fresh_sums)
        lines = lines + core_swap(lines)
        reward = sum_in_turn(lines).reshape(8 * row_count, STEPS)
        wanted = f * (8 * CAP) + jnp.arange(8 * CAP, dtype=jnp.int32)
        hits = slots_all[None, :] == wanted[:, None].astype(jnp.float32)
        step_rewards = jnp.sum(jnp.where(hits[:, :, None], reward[None], 0.0), axis=1)
        head_grad = jnp.transpose(returned.reshape(4 * units, wide)).astype(jnp.float32)
        return step_rewards, head_grad

    main_batch = (main_spots, scored(main_parts, main_spots))
    if LOCAL == tokens_most:
        return rest_of([main_batch])

    def with_more():
        more_parts, more_spots, _, _ = gathered(LOCAL, tokens_most - LOCAL)
        return rest_of([main_batch, (more_spots, scored(more_parts, more_spots))])

    return lax.cond(overflow, with_more, lambda: rest_of([main_batch]))


def solution(mesh):
    in_specs = (
        P("fsdp", None, None),
        P("fsdp", None),
        P("fsdp"),
        P("fsdp", None),
        P("fsdp", None),
        P(),
        P("fsdp", "rep"),
        P("rep"),
    )
    out_specs = (P("fsdp", None), P("fsdp", "rep"))

    def local(states, *rest):
        if lax.axis_size("rep") == 4 and lax.axis_size("fsdp") == 8:
            return spread_tokens(states, *rest)
        return gathered_weights(states, *rest)

    return jax.shard_map(local, mesh=mesh, in_specs=in_specs, out_specs=out_specs, check_vma=False)
```

```python
import functools
import math

import jax
import jax.numpy as jnp
from jax import lax
from jax.experimental import pallas as pl
from jax.experimental.pallas import tpu as pltpu
from jax.sharding import PartitionSpec as P

CAP = 2
STEPS = 8
LOCAL = 384
VMEM_BYTES = 52 * 1024 * 1024


def silu_slope(pre_act):
    sigma = jax.nn.sigmoid(pre_act)
    return sigma * (1.0 + pre_act * (1.0 - sigma))


def normalize(tokens_flat, gain):
    wide = tokens_flat.astype(jnp.float32)
    meansq = jnp.mean(wide * wide, axis=1, keepdims=True)
    return (wide * lax.rsqrt(meansq + 1e-06) * gain[None, :]).astype(jnp.bfloat16)


def member_of(segments, lengths):
    positions = jnp.arange(segments.shape[1], dtype=jnp.int32)
    valid = (positions[None, :] < lengths[:, None]).astype(jnp.float32)
    step_ids = jnp.arange(STEPS, dtype=jnp.int32)
    return (segments[:, :, None] == step_ids[None, None, :]).astype(jnp.float32) * valid[:, :, None]


def rank_of(target):
    order = jnp.arange(target.shape[0], dtype=jnp.int32)
    earlier = (target[:, None] == target[None, :]) & (order[None, :] < order[:, None])
    return jnp.sum(earlier.astype(jnp.int32), axis=1)


def gathered_weights(states, labels, lengths, segments, destinations, gain, head_in, head_out):
    row_count, slot_span, feature_width = states.shape
    trainers = lax.axis_size("fsdp")
    slot_total = trainers * CAP
    normed = normalize(states.reshape(-1, feature_width), gain)
    member = member_of(segments, lengths)
    live = jnp.max(member, axis=1)

    def scored(weights):
        pre_act = jnp.dot(normed, weights, preferred_element_type=jnp.float32)
        partial = jnp.sum(jax.nn.silu(pre_act) * head_out[None, :], axis=1)
        return pre_act, lax.psum(partial, "rep").reshape(row_count, slot_span)

    pre_act, score = scored(lax.all_gather(head_in, "fsdp", axis=0, tiled=True))
    step_score = jnp.einsum("rs,rsk->rk", score, member, precision=lax.Precision.HIGHEST)
    step_error = live * (step_score - labels.astype(jnp.float32))
    token_error = jnp.einsum("rk,rsk->rs", step_error, member, precision=lax.Precision.HIGHEST).reshape(-1)
    pre_grad = (token_error[:, None] * head_out[None, :] * silu_slope(pre_act)).astype(jnp.bfloat16)
    rate = 0.5 / math.sqrt(row_count * trainers * slot_span)
    head_grad = lax.psum_scatter(
        lax.dot_general(normed, pre_grad, (((0,), (0,)), ((), ())), preferred_element_type=jnp.float32),
        "fsdp",
        scatter_dimension=0,
        tiled=True,
    )
    fresh = (head_in.astype(jnp.float32) - rate * head_grad).astype(jnp.bfloat16)
    _, fresh_score = scored(lax.all_gather(fresh, "fsdp", axis=0, tiled=True))
    reward = jnp.einsum("rs,rsk->rk", fresh_score, member, precision=lax.Precision.HIGHEST)
    target = destinations[:, 0]
    slot = target * CAP + rank_of(target)
    placing = (slot[None, :] == jnp.arange(slot_total, dtype=jnp.int32)[:, None]).astype(jnp.float32)
    placed = jnp.dot(placing, reward, precision=lax.Precision.HIGHEST)
    return lax.all_to_all(placed, "fsdp", split_axis=0, concat_axis=0, tiled=True), head_grad


X_MATE = [(r, r ^ 1) for r in range(4)]
Y_MATE = [(r, r ^ 2) for r in range(4)]
XY_MATE = [(r, r ^ 3) for r in range(4)]
CORE_MATE = [(f, f ^ 1) for f in range(8)]
Z1_MATE = [(f, f ^ 2) for f in range(8)]
Z2_MATE = [(f, f ^ 4) for f in range(8)]
Z3_MATE = [(f, f ^ 6) for f in range(8)]
INNER = [(f, f ^ 6) for f in (2, 3, 4, 5)]
OUTWARD = [(f, f ^ 2) for f in (2, 3, 4, 5)]


def sum_over_chips(values):
    values = (values + lax.ppermute(values, "rep", X_MATE)) + (
        lax.ppermute(values, "rep", Y_MATE) + lax.ppermute(values, "rep", XY_MATE)
    )
    return (values + lax.ppermute(values, "fsdp", Z1_MATE)) + (
        lax.ppermute(values, "fsdp", Z2_MATE) + lax.ppermute(values, "fsdp", Z3_MATE)
    )


def core_swap(values):
    return lax.ppermute(values, "fsdp", CORE_MATE)


def sum_in_turn(values):
    for axis, pairs in (("rep", X_MATE), ("rep", Y_MATE), ("fsdp", Z1_MATE), ("fsdp", Z2_MATE)):
        values = values + lax.ppermute(values, axis, pairs)
    return values


def gather_small(values):
    copies = jnp.broadcast_to(values[None], (8,) + values.shape)
    return lax.all_to_all(copies, "fsdp", split_axis=0, concat_axis=0, tiled=True)


def around(part, own, inner, weights=None, facts=None):
    half = part.shape[0] // 32 * 16
    together = lax.optimization_barrier

    def along(values, pairs):
        return lax.ppermute(values, "fsdp", pairs)

    def x_of(values):
        return lax.ppermute(values, "rep", X_MATE)

    def y_of(values):
        return lax.ppermute(values, "rep", Y_MATE)

    a, b_in = together((along(part, Z1_MATE), along(part, INNER)))
    own, a = together((own, a))
    second = (x_of(a), y_of(a), along(b_in, OUTWARD), along(a, INNER))
    if facts is not None:
        facts = gather_small(facts)
        second, facts = together((second, facts))
    ax, ay, b_out, c_in = together(second)
    b = jnp.where(inner, b_in, b_out)
    c_out = along(c_in, OUTWARD)
    if weights is not None:
        weights, ax = together((weights, ax))
        weights = lax.all_to_all(
            jnp.transpose(weights).reshape(4, -1, weights.shape[0]),
            "fsdp",
            0,
            0,
            axis_index_groups=[[0, 2, 4, 6], [1, 3, 5, 7]],
            tiled=True,
        )
    a_low, a_high, bx, by = together((y_of(ax[:half]), x_of(ay[half:]), x_of(b), y_of(b)))
    c_out, bx = together((c_out, bx))
    c = jnp.where(inner, c_in, c_out)
    fourth = (y_of(bx[:half]), x_of(by[half:]), x_of(c), y_of(c))
    if weights is not None:
        fourth, weights = together((fourth, weights))
    b_low, b_high, cx, cy = together(fourth)
    c_low, c_high = y_of(cx[:half]), x_of(cy[half:])
    parts = [own, a, ax, ay, a_low, a_high, b, bx, by, b_low, b_high, c, cx, cy, c_low, c_high]
    return parts, weights, facts


def step_sums(pre, share, spots, bounds_ref, sums_ref):
    score = jnp.sum(pre * jax.nn.sigmoid(pre) * share, axis=0, keepdims=True)
    span = spots.shape[2]
    for at in range(spots.shape[0]):
        here = spots[at]
        low = bounds_ref[at, :, 0:1]
        high = bounds_ref[at, :, 1:2]
        inside = (here >= low) & (here < high)
        sums = jnp.sum(jnp.where(inside, score[:, at * span : (at + 1) * span], 0.0), axis=1, keepdims=True)
        sums_ref[at] = jnp.broadcast_to(sums, sums_ref.shape[1:])


def first_kernel(offsets_ref, *refs, sizes, blocks, first, carried):
    count = len(sizes)
    parts = refs[:count]
    own_w, mate_w, share_ref, spots_ref, bounds_ref = refs[count : count + 5]
    outs = refs[count + 5 + carried :]
    sums_ref, pre_ref, kept_ref, given_ref, x_s, w_s, acc_s, in_sem, w_sem, out_sem = outs
    wide = own_w.shape[2]
    tile, width = x_s.shape
    depth = width // blocks
    loads = []
    for j in range(blocks):
        columns = pl.ds(j * depth, depth)
        here = []
        for core, source in enumerate((own_w, mate_w)):
            where = pl.ds(pl.multiple_of(offsets_ref[core * 4 + j], 128), wide)
            here.append(pltpu.make_async_copy(source.at[j], w_s.at[:, where], w_sem.at[core * 4 + j]))
        at = 0
        for index, size in enumerate(sizes):
            here.append(
                pltpu.make_async_copy(
                    parts[index].at[:, columns], x_s.at[pl.ds(at, size), columns], in_sem.at[j, index]
                )
            )
            at += size
        loads.append(here)
    for here in loads:
        for copy in here:
            copy.start()
    rows = pl.ds(first, tile)
    out_copies = []
    for j in range(blocks):
        for copy in loads[j]:
            copy.wait()
        for core, dest in enumerate((kept_ref, given_ref)):
            where = pl.ds(pl.multiple_of(offsets_ref[core * 4 + j], 128), wide)
            out_copies.append(
                pltpu.make_async_copy(x_s.at[:, where], dest.at[j, rows], out_sem.at[core * 4 + j])
            )
            out_copies[-1].start()
        columns = pl.ds(j * depth, depth)
        term = lax.dot_general(
            w_s[:, columns], x_s[:, columns], (((1,), (1,)), ((), ())), preferred_element_type=jnp.float32
        )
        if j == 0:
            acc_s[...] = term
        else:
            acc_s[...] += term

    out_copies.append(pltpu.make_async_copy(acc_s, pre_ref.at[:, rows], out_sem.at[8]))
    out_copies[-1].start()
    step_sums(acc_s[...], share_ref[...], spots_ref[...], bounds_ref, sums_ref)
    for copy in out_copies:
        copy.wait()


def first_scores(parts, own_w, mate_w, share, spots, bounds, offsets, first, chips, carried=()):
    sizes = tuple(part.shape[0] for part in parts)
    tile = sum(sizes)
    width = parts[0].shape[1]
    units, wide = own_w.shape[1:]
    anywhere = pl.BlockSpec(memory_space=pl.ANY)
    vmem = pl.BlockSpec(memory_space=pltpu.VMEM)
    here = slice(first, first + chips)
    total = tile // chips * 4
    first_carried = 1 + len(parts) + 5
    return pl.pallas_call(
        functools.partial(first_kernel, sizes=sizes, blocks=4, first=first * (tile // chips), carried=len(carried)),
        out_shape=(
            jax.ShapeDtypeStruct((chips, bounds.shape[1], 128), jnp.float32),
            jax.ShapeDtypeStruct((units, total), jnp.float32),
            jax.ShapeDtypeStruct((4, total, wide), jnp.bfloat16),
            jax.ShapeDtypeStruct((4, total, wide), jnp.bfloat16),
        ),
        in_specs=[pl.BlockSpec(memory_space=pltpu.SMEM)]
        + [anywhere] * (len(parts) + 2)
        + [vmem] * 3
        + [anywhere] * len(carried),
        out_specs=(vmem, anywhere, anywhere, anywhere),
        input_output_aliases={first_carried + i: 1 + i for i in range(len(carried))},
        scratch_shapes=[
            pltpu.VMEM((tile, width), jnp.bfloat16),
            pltpu.VMEM((units, width), jnp.bfloat16),
            pltpu.VMEM((units, tile), jnp.float32),
            pltpu.SemaphoreType.DMA((4, len(parts))),
            pltpu.SemaphoreType.DMA((8,)),
            pltpu.SemaphoreType.DMA((9,)),
        ],
        compiler_params=pltpu.CompilerParams(vmem_limit_bytes=VMEM_BYTES),
        cost_estimate=pl.CostEstimate(
            flops=2 * units * width * tile, bytes_accessed=4 * tile * width, transcendentals=units * tile
        ),
        name="first_scores",
    )(offsets, *parts, own_w, mate_w, share, spots[here], bounds[here], *carried)


def fresh_kernel(kept_ref, given_ref, own_w, mate_w, share_ref, spots_ref, bounds_ref, sums_ref, acc_s):
    half = pl.program_id(0)
    k = pl.program_id(1)
    contract = (((1,), (1,)), ((), ()))
    term = lax.dot_general(own_w[0], kept_ref[0], contract, preferred_element_type=jnp.float32)
    term = term + lax.dot_general(mate_w[0], given_ref[0], contract, preferred_element_type=jnp.float32)

    @pl.when(k == 0)
    def _():
        acc_s[...] = term

    @pl.when(k > 0)
    def _():
        acc_s[...] += term

    @pl.when(k == 3)
    def _():
        step_sums(acc_s[...], share_ref[...], spots_ref[...], bounds_ref, sums_ref)


def fresh_scores(kept, given, own_w, mate_w, share, spots, bounds):
    total, wide = kept.shape[1:]
    units = own_w.shape[1]
    steps = bounds.shape[1]
    tile = total // 2
    tokens = pl.BlockSpec((1, tile, wide), lambda h, k: (k, h, 0))
    weights = pl.BlockSpec((1, units, wide), lambda h, k: (k, 0, 0))
    return pl.pallas_call(
        fresh_kernel,
        grid=(2, 4),
        out_shape=jax.ShapeDtypeStruct((4, steps, 128), jnp.float32),
        in_specs=[
            tokens,
            tokens,
            weights,
            weights,
            pl.BlockSpec((units, 1), lambda h, k: (0, 0)),
            pl.BlockSpec((2,) + spots.shape[1:], lambda h, k: (h, 0, 0)),
            pl.BlockSpec((2, steps, 2), lambda h, k: (h, 0, 0)),
        ],
        out_specs=pl.BlockSpec((2, steps, 128), lambda h, k: (h, 0, 0)),
        scratch_shapes=[pltpu.VMEM((units, tile), jnp.float32)],
        compiler_params=pltpu.CompilerParams(vmem_limit_bytes=VMEM_BYTES),
        cost_estimate=pl.CostEstimate(
            flops=4 * units * wide * 4 * total, bytes_accessed=16 * total * wide, transcendentals=units * total
        ),
        name="fresh_scores",
    )(kept, given, own_w, mate_w, share, spots, bounds)


def grad_kernel(rate, count, *refs):
    head_ref = refs[0]
    ins = refs[1 : 1 + 2 * count]
    grad_ref, fresh_ref = refs[1 + 2 * count :]
    grad = jnp.dot(ins[0][...], ins[1][0], preferred_element_type=jnp.float32)
    for at in range(2, 2 * count, 2):
        grad = grad + jnp.dot(ins[at][...], ins[at + 1][0], preferred_element_type=jnp.float32)
    grad_ref[0] = grad.astype(grad_ref.dtype)
    fresh_ref[0] = (head_ref[0].astype(jnp.float32) - rate * grad).astype(fresh_ref.dtype)


def grads_and_fresh(head, terms, rate):
    units, wide = head.shape[1:]
    block = pl.BlockSpec((1, units, wide), lambda j: (j, 0, 0))
    specs = [block]
    flat = [head]
    work = 0
    for pre_grad, tokens in terms:
        specs.append(pl.BlockSpec(pre_grad.shape, lambda j: (0, 0)))
        specs.append(pl.BlockSpec((1,) + tokens.shape[1:], lambda j: (j, 0, 0)))
        flat += [pre_grad, tokens]
        work += tokens.size
    return pl.pallas_call(
        functools.partial(grad_kernel, rate, len(terms)),
        grid=(4,),
        out_shape=(jax.ShapeDtypeStruct(head.shape, jnp.bfloat16),) * 2,
        in_specs=specs,
        out_specs=(block, block),
        compiler_params=pltpu.CompilerParams(vmem_limit_bytes=VMEM_BYTES),
        cost_estimate=pl.CostEstimate(flops=2 * units * work, bytes_accessed=2 * work, transcendentals=0),
        name="grads_and_fresh",
    )(*flat)


def spread_tokens(states, labels, lengths, segments, destinations, gain, head_in, head_out):
    row_count, slot_span, width = states.shape
    tokens_most = row_count * slot_span
    f = lax.axis_index("fsdp")
    r = lax.axis_index("rep")
    z = f // 2
    c = f % 2
    inner = (z == 1) | (z == 2)
    units = head_in.shape[1] // 4
    wide = head_in.shape[0]
    flat_states = states.reshape(-1, width)

    row_ids = jnp.arange(row_count)
    ends_row = jnp.sum(jnp.where(row_ids[:, None] >= row_ids[None, :], lengths[None, :], 0), axis=1)
    place = jnp.where(
        jnp.arange(slot_span)[None, :] < lengths[:, None],
        (ends_row - lengths)[:, None] + jnp.arange(slot_span)[None, :],
        -1,
    ).reshape(-1)

    def compacted(first, count):
        spots = first + jnp.arange(count, dtype=jnp.int32)
        picks = (place[None, :] == spots[:, None]).astype(jnp.bfloat16)
        tokens = jnp.dot(picks, flat_states, preferred_element_type=jnp.float32)
        return normalize(tokens.astype(jnp.bfloat16), gain)

    def gathered(first, count, weights=None, facts=None):
        quarter = count // 4
        mine = compacted(first + r * quarter, quarter)
        parts, weights, facts = around(mine, compacted(first, count), inner, weights, facts)
        plain = (first + jnp.arange(count))[None, :]
        moved = jnp.concatenate([first + (r ^ j) * quarter + jnp.arange(quarter) for j in range(4)])[None, :]
        spots = jnp.stack([plain, moved, moved, moved]).astype(jnp.float32)
        return parts, spots, weights, facts

    counts = jnp.sum(member_of(segments, lengths), axis=1)
    target = destinations[:, 0]
    slot_of = target * (8 * CAP) + f * CAP + rank_of(target)
    facts = jnp.concatenate(
        [counts.reshape(-1), labels.astype(jnp.float32).reshape(-1), slot_of.astype(jnp.float32)]
    )
    facts = jnp.pad(facts, (0, 384 - facts.shape[0]))
    main_parts, main_spots, own_head, facts_all = gathered(0, LOCAL, head_in, facts)
    steps = row_count * STEPS
    counts_all = facts_all[:, :steps]
    labels_all = facts_all[:, steps : 2 * steps]
    slots_all = facts_all[:, 2 * steps : 2 * steps + row_count].reshape(-1)
    upto = jnp.arange(steps)[:, None] >= jnp.arange(steps)[None, :]
    ends_all = jnp.sum(jnp.where(upto[None], counts_all[:, None, :], 0.0), axis=2)
    lows_all = ends_all - counts_all
    overflow = jnp.max(ends_all[:, steps - 1]) > LOCAL

    sources = [z, z ^ 1, jnp.where(z < 2, 2, 1), jnp.where(z < 2, 3, 0)]
    takes = [jnp.arange(8) == source * 2 + c for source in sources]

    def of_chips(values):
        return jnp.stack([jnp.sum(jnp.where(take[:, None], values, 0.0), axis=0) for take in takes])

    bounds = jnp.stack([of_chips(lows_all), of_chips(ends_all)], axis=2)
    labels_here = of_chips(labels_all)
    live_here = jnp.minimum(of_chips(counts_all), 1.0)

    def of_lines(chip_sums):
        return sum(jnp.where(take[:, None], chip_sums[i][None, :], 0.0) for i, take in enumerate(takes))

    mate_head = core_swap(own_head)
    share = lax.dynamic_slice_in_dim(head_out, z * units, units)[:, None]
    rate = 0.5 / math.sqrt(row_count * 8 * slot_span)
    blocks_at = [(j * 2 + core) * wide for core in (c, 1 - c) for j in range(4)]
    offsets = jnp.stack(blocks_at).astype(jnp.int32)

    def scored(parts, spots):
        facts_of = (own_head, mate_head, share, spots, bounds, offsets)
        near_sums, *carried = first_scores(parts[:6], *facts_of, 0, 2)
        last_sums, *carried = first_scores(parts[6:], *facts_of, 2, 2, carried)
        return (jnp.concatenate([near_sums, last_sums]), *carried)

    def pre_grad_of(pre, spots, step_error):
        errors = []
        for i in range(4):
            inside = (spots[i] >= bounds[i, :, 0:1]) & (spots[i] < bounds[i, :, 1:2])
            errors.append(jnp.sum(jnp.where(inside, step_error[i][:, None], 0.0), axis=0))
        return (jnp.concatenate(errors)[None, :] * share * silu_slope(pre)).astype(jnp.bfloat16)

    def rest_of(batches):
        chip_sums = sum(sums[:, :, 0] for _, (sums, _, _, _) in batches)
        step_score = of_chips(sum_over_chips(of_lines(chip_sums)))
        step_error = live_here * (step_score - labels_here)
        terms = []
        for spots, (_, pre, kept, given) in batches:
            pre_grad = pre_grad_of(pre, spots, step_error)
            terms += [(pre_grad, kept), (core_swap(pre_grad), core_swap(given))]
        grads, own_fresh = grads_and_fresh(own_head, terms, rate)
        returned = lax.all_to_all(
            grads, "fsdp", 0, 0, axis_index_groups=[[0, 2, 4, 6], [1, 3, 5, 7]], tiled=True
        )
        mate_fresh = core_swap(own_fresh)
        fresh_sums = sum(
            fresh_scores(kept, given, own_fresh, mate_fresh, share, spots, bounds)[:, :, 0]
            for spots, (_, _, kept, given) in batches
        )
        lines = of_lines(fresh_sums)
        lines = lines + core_swap(lines)
        reward = sum_in_turn(lines).reshape(8 * row_count, STEPS)
        wanted = f * (8 * CAP) + jnp.arange(8 * CAP, dtype=jnp.int32)
        hits = slots_all[None, :] == wanted[:, None].astype(jnp.float32)
        step_rewards = jnp.sum(jnp.where(hits[:, :, None], reward[None], 0.0), axis=1)
        head_grad = jnp.transpose(returned.reshape(4 * units, wide)).astype(jnp.float32)
        return step_rewards, head_grad

    main_batch = (main_spots, scored(main_parts, main_spots))
    if LOCAL == tokens_most:
        return rest_of([main_batch])

    def with_more():
        more_parts, more_spots, _, _ = gathered(LOCAL, tokens_most - LOCAL)
        return rest_of([main_batch, (more_spots, scored(more_parts, more_spots))])

    return lax.cond(overflow, with_more, lambda: rest_of([main_batch]))


def solution(mesh):
    in_specs = (
        P("fsdp", None, None),
        P("fsdp", None),
        P("fsdp"),
        P("fsdp", None),
        P("fsdp", None),
        P(),
        P("fsdp", "rep"),
        P("rep"),
    )
    out_specs = (P("fsdp", None), P("fsdp", "rep"))

    def local(states, *rest):
        if lax.axis_size("rep") == 4 and lax.axis_size("fsdp") == 8:
            return spread_tokens(states, *rest)
        return gathered_weights(states, *rest)

    return jax.shard_map(local, mesh=mesh, in_specs=in_specs, out_specs=out_specs, check_vma=False)
```
